512 devices in a mesh: tm: 16 (over y, core), space: 32 (over z, x).
Axes of the slice: x: 4, y: 8, z: 8, core: 2. Of those that a mesh axis runs over, the one named last changes fastest.
Arguments:
- iterate: float32 [64, 256, 2048], P('tm', 'space'), may hold values from -8 to 8
- initial: float32 [256, 2048], P('space'), may hold values from -6 to 6
- diffusion: float32 [256, 2048], P('space'), may hold values from 0.05 to 0.5
- courant_x: float32 [256, 2048], P('space'), may hold values from -1 to 1
- courant_y: float32 [256, 2048], P('space'), may hold values from -4 to 4
Outputs:
- new_iterate: float32 [64, 256, 2048], P('tm', 'space')
The draws below stay inside these ranges and needn't reach their ends.
All inputs are finite; a program needn't handle non-finite values.
Results may differ from the reference program's by a relative error of at most 0.0003.
Values sent between devices are 32-bit elements; how exact they have to be, the bound alone decides.
No kernel may reach another device: no remote copies, remote signals or barrier semaphores. Data moves between devices by JAX's collectives and lax.ppermute only.
A program may use at most 64 MiB of HBM per device.

```python
import math
import jax
import jax.numpy as jnp
from jax import lax

STEPS = 64
NX = 2048
NY = 256
SWEEPS = 8


def draw_iterate(key, part):
    key = jax.random.fold_in(key, 7)
    roughness = jax.random.truncated_normal(key, -6.0, 6.0, (STEPS, NY, NX), jnp.float32)
    return roughness


def block_scale(own_key, dims, split, least, high):
    level = 1.0
    for axis_at, parts in split:
        draws = jax.random.uniform(jax.random.fold_in(jax.random.fold_in(own_key, 6), axis_at), (parts,), jnp.float32, least / len(split), high / len(split))
        level = level * jnp.repeat(jnp.exp(draws), dims[axis_at] // parts).reshape((-1,) + (1,) * (len(dims) - 1 - axis_at))
    return level


def centred(own_key, shape, scale, most, shards=(), held_as=jnp.bfloat16):
    factor_of = block_scale(own_key, shape, shards, -0.22, 0.18) if shards else 1.0
    values = jax.random.normal(own_key, shape, jnp.float32) * scale * factor_of
    return jnp.minimum(jnp.maximum(values, -most), most).astype(held_as)


def setup_inputs(seed: int = 0) -> dict:
    streams_of = jax.random.split(jax.random.key(seed), 6)
    return {
        "iterate": draw_iterate(jax.random.fold_in(streams_of[5], 71), 0),
        "initial": centred(streams_of[1], (NY, NX), 1.0, 6.0, ((0, 32),), jnp.float32),
        "diffusion": jnp.clip(jnp.exp(math.log(0.5) - 2.3025851 * jax.random.uniform(streams_of[2], (NY, NX), jnp.float32) ** block_scale(streams_of[2], (NY, NX), ((0, 32),), -0.2, 0.2)), 0.05, 0.5),
        "courant_x": jnp.clip(jax.random.uniform(streams_of[3], (NY, NX), jnp.float32, -1.0, 1.0) * block_scale(streams_of[3], (NY, NX), ((0, 32),), -0.4, 0.0), -1.0, 1.0),
        "courant_y": jnp.clip(jax.random.uniform(streams_of[4], (NY, NX), jnp.float32, -4.0, 4.0) * block_scale(streams_of[4], (NY, NX), ((0, 32),), -0.4, 0.0), -4.0, 4.0),
    }


alpha_ratio = 0.01


def exact_dot(left, right):
    return jnp.dot(left, right, precision=lax.Precision.HIGHEST, preferred_element_type=jnp.float32)


def stencil_weights(diffusion, courant_x, courant_y):
    west_weight = diffusion + jnp.maximum(courant_x, 0.0)
    east_weight = diffusion + jnp.maximum(-courant_x, 0.0)
    north_weight = diffusion + jnp.maximum(courant_y, 0.0)
    south_weight = diffusion + jnp.maximum(-courant_y, 0.0)
    return west_weight, east_weight, north_weight, south_weight


def neighbours(padded, stencil):
    summed = stencil[0] * padded[..., 1:-1, :-2] + stencil[1] * padded[..., 1:-1, 2:]
    return summed + stencil[2] * padded[..., :-2, 1:-1] + stencil[3] * padded[..., 2:, 1:-1]


def time_tables(length):
    indices = jnp.arange(length, dtype=jnp.int32)
    product_index = (indices[:, None] * indices[None, :]) % length
    angles = (2.0 * math.pi / length) * product_index.astype(jnp.float32)
    scaling = jnp.power(alpha_ratio, indices.astype(jnp.float32) / length)
    fwd_real = jnp.cos(angles) * scaling[None, :]
    fwd_imag = -jnp.sin(angles) * scaling[None, :]
    inv_real = jnp.cos(angles) / (length * scaling[:, None])
    inv_imag = -jnp.sin(angles) / (length * scaling[:, None])
    return fwd_real, fwd_imag, inv_real, inv_imag


def frequency_shifts(freq_index, length):
    angles = (2.0 * math.pi / length) * freq_index.astype(jnp.float32)
    beta_value = alpha_ratio ** (1.0 / length)
    return 1.0 - beta_value * jnp.cos(angles), beta_value * jnp.sin(angles)


def reference(iterate, initial, diffusion, courant_x, courant_y):
    stencil = stencil_weights(diffusion, courant_x, courant_y)
    centre = stencil[0] + stencil[1] + stencil[2] + stencil[3]
    earlier = jnp.concatenate([initial[None], iterate[:STEPS - 1]], 0)
    padded = jnp.pad(iterate, ((0, 0), (1, 1), (1, 1)))
    residual = earlier - iterate + neighbours(padded, stencil) - centre * iterate
    fwd_real, fwd_imag, inv_real, inv_imag = time_tables(STEPS)
    flattened = residual.reshape(STEPS, -1)
    hat_real = exact_dot(fwd_real, flattened).reshape(residual.shape)
    hat_imag = exact_dot(fwd_imag, flattened).reshape(residual.shape)
    lam_real, lam_imag = frequency_shifts(jnp.arange(STEPS, dtype=jnp.int32), STEPS)

    def solve_one(frequency_item):
        f_real, f_imag, shift_real, shift_imag = frequency_item
        diag_real = shift_real + centre
        diag_imag = shift_imag
        inverse_norm = 1.0 / (diag_real * diag_real + diag_imag * diag_imag)
        sol_real = (f_real * diag_real + f_imag * diag_imag) * inverse_norm
        sol_imag = (f_imag * diag_real - f_real * diag_imag) * inverse_norm
        for sweep_index in range(SWEEPS - 1):
            q_real = f_real + neighbours(jnp.pad(sol_real, 1), stencil)
            q_imag = f_imag + neighbours(jnp.pad(sol_imag, 1), stencil)
            sol_real = (q_real * diag_real + q_imag * diag_imag) * inverse_norm
            sol_imag = (q_imag * diag_real - q_real * diag_imag) * inverse_norm
        return sol_real, sol_imag

    sol_real, sol_imag = lax.map(solve_one, (hat_real, hat_imag, lam_real, lam_imag))
    correction = exact_dot(inv_real, sol_real.reshape(STEPS, -1)) + exact_dot(inv_imag, sol_imag.reshape(STEPS, -1))
    return iterate + correction.reshape(iterate.shape)
```

```python
import math

import jax
import jax.numpy as jnp
import numpy as np
from jax import lax
from jax.experimental import pallas as pl
from jax.experimental.pallas import tpu as pltpu
from jax.sharding import PartitionSpec as P

SWEEPS = 8
ALPHA = 0.01
STEPS = 64
HALF = STEPS // 2
DEVS = 16
LOCAL = STEPS // DEVS
ROWS = 8
LANES = 128
BLOCK = ROWS * LOCAL + ROWS
SPAN = 3 * ROWS
WIDE = 2 * LANES
F32 = jnp.float32


def tables():
    n = np.arange(STEPS)
    g = ALPHA ** (n / STEPS)
    k = np.arange(HALF)
    ang = 2.0 * np.pi * (np.outer(k, n) % STEPS) / STEPS
    fwd = np.concatenate([np.cos(ang) * g, -np.sin(ang) * g], 0)
    fwd[HALF] = (-1.0) ** n * g
    inv = np.concatenate([2.0 * np.cos(ang), -2.0 * np.sin(ang)], 0).T
    inv[:, 0] = 1.0
    inv[:, HALF] = (-1.0) ** n
    inv = inv / (STEPS * g[:, None])
    beta = ALPHA ** (1.0 / STEPS)
    shift_re = 1.0 - beta * np.cos(2.0 * np.pi * k / STEPS)
    shift_im = beta * np.sin(2.0 * np.pi * k / STEPS)
    shift_alt = shift_re.copy()
    shift_alt[0] = 1.0 + beta
    shifts = np.zeros((HALF, 3 * LANES), np.float32)
    shifts[:, :LANES] = shift_re[:, None]
    shifts[:, LANES : 2 * LANES] = shift_im[:, None]
    shifts[:, 2 * LANES :] = shift_alt[:, None]
    return fwd.astype(np.float32), inv.astype(np.float32), shifts


def lane_ids(rows):
    return lax.broadcasted_iota(jnp.int32, (rows, LANES), 1)


def rim(left, right):
    lane = lane_ids(ROWS)
    both = jnp.where(lane < 8, right, jnp.where(lane >= LANES - 8, left, 0.0))
    moved = pltpu.roll(both, 8, 1, stride=16, stride_axis=0)
    return jnp.sum(moved, axis=0, keepdims=True)


def pack_kernel(t_ref, it_ref, ini_ref, dif_ref, cx_ref, cy_ref, send_ref, coef_ref):
    zero = jnp.zeros((ROWS, LANES), F32)
    for d in range(DEVS):
        rims = []
        for n in range(LOCAL):
            cols = lambda e: it_ref[n, :, e * LANES : (e + 1) * LANES]
            send_ref[d, n * ROWS : (n + 1) * ROWS, :] = cols(d)
            rims.append(rim(cols(d - 1) if d else zero, cols(d + 1) if d + 1 < DEVS else zero))
        rims.append(jnp.zeros((ROWS - LOCAL, LANES), F32))
        send_ref[d, LOCAL * ROWS :, :] = jnp.concatenate(rims, 0)
    t = t_ref[0]
    rims = []
    for a, ref in enumerate((ini_ref, dif_ref, cx_ref, cy_ref)):
        cols = lambda e: ref[:, pl.ds(pl.multiple_of(e * LANES, LANES), LANES)]
        coef_ref[a * ROWS : (a + 1) * ROWS, :] = cols(t)
        left = jnp.where(t > 0, cols(jnp.maximum(t - 1, 0)), 0.0)
        right = jnp.where(t < DEVS - 1, cols(jnp.minimum(t + 1, DEVS - 1)), 0.0)
        rims.append(rim(left, right))
    rims.append(jnp.zeros((ROWS - LOCAL, LANES), F32))
    coef_ref[LOCAL * ROWS :, :] = jnp.concatenate(rims, 0)


def mul(matrix, value):
    return jnp.dot(matrix, value, precision=lax.Precision.HIGHEST, preferred_element_type=F32)


def solve_kernel(
    fwd_ref, inv_ref, shift_ref, up_ref, own_ref, dn_ref, cup_ref, cown_ref, cdn_ref,
    out_ref, x_ref, rim_ref, side_ref, wt_ref, a_ref, alt_ref, b_ref, f_ref, w_ref, v_ref,
):
    lane = lane_ids(1)
    inside = (lane < 8) | (lane >= LANES - 8)
    for blk, (ref, cref) in enumerate(((up_ref, cup_ref), (own_ref, cown_ref), (dn_ref, cdn_ref))):
        for d in range(DEVS):
            rim_ref[d * LOCAL : (d + 1) * LOCAL, :] = ref[d * BLOCK + LOCAL * ROWS : d * BLOCK + LOCAL * ROWS + LOCAL, :]
        rims = rim_ref[...]
        for r in range(ROWS):
            j = blk * ROWS + r
            for d in range(DEVS):
                x_ref[j, 8 + d * LOCAL : 8 + (d + 1) * LOCAL, :LANES] = ref[pl.ds(d * BLOCK + r, LOCAL, stride=ROWS), :]
            turned = pltpu.roll(rims, (2 * LANES - 16 * r - 8) % LANES, 1)
            x_ref[j, 8:, LANES:] = jnp.where(inside, turned, 0.0)
            turned = pltpu.roll(cref[LOCAL * ROWS :, :], (2 * LANES - 16 * r - 8) % LANES, 1)
            turned = jnp.where(inside, turned, 0.0)
            x_ref[j, 7:8, :LANES] = cref[r : r + 1, :]
            x_ref[j, 7:8, LANES:] = turned[0:1]
            for a in (1, 2, 3):
                side_ref[a, r : r + 1, :] = turned[a : a + 1]
        wide = []
        for a in (1, 2, 3):
            wide.append(jnp.concatenate([cref[a * ROWS : (a + 1) * ROWS, :], side_ref[a]], 1))
        dif, cx, cy = wide
        west = dif + jnp.maximum(cx, 0.0)
        east = dif + jnp.maximum(-cx, 0.0)
        north = dif + jnp.maximum(cy, 0.0)
        south = dif + jnp.maximum(-cy, 0.0)
        rows = slice(blk * ROWS, (blk + 1) * ROWS)
        for a, value in enumerate((west, east, north, south, west + east + north + south)):
            wt_ref[a, rows, :] = value

    def weights(j):
        return [wt_ref[a, pl.ds(j, 1), :] for a in range(5)]

    def near(wts, here, above, below):
        summed = wts[0] * pltpu.roll(here, 1, 1) + wts[1] * pltpu.roll(here, WIDE - 1, 1)
        return summed + wts[2] * above + wts[3] * below

    def first(j, carry):
        wts = weights(j)
        here = x_ref[j, 8:, :]
        r = x_ref[j, 7 : 7 + STEPS, :] - here + near(wts, here, x_ref[j - 1, 8:, :], x_ref[j + 1, 8:, :]) - wts[4] * here
        hat = mul(fwd_ref[...], r)
        for g in range(HALF // 8):
            part = slice(8 * g, 8 * g + 8)
            h_re, h_im = hat[8 * g : 8 * g + 8], hat[HALF + 8 * g : HALF + 8 * g + 8]
            rep = lambda c: jnp.concatenate([shift_ref[part, c * LANES : (c + 1) * LANES]] * 2, 1)
            s_im = rep(1)
            d_re = rep(0) + wts[4]
            norm = 1.0 / (d_re * d_re + s_im * s_im)
            a_re = d_re * norm
            a_im = a_re
            b = s_im * norm
            if g == 0:
                d_im = rep(2) + wts[4]
                a_im = d_im * (1.0 / (d_im * d_im + s_im * s_im))
                alt_ref[j] = a_im
            a_ref[j, part, :] = a_re
            b_ref[j, part, :] = b
            w_re = h_re * a_re + h_im * b
            w_im = h_im * a_im - h_re * b
            f_ref[j, part, :] = w_re
            f_ref[j, HALF + 8 * g : HALF + 8 * g + 8, :] = w_im
        return carry

    lax.fori_loop(1, SPAN - 1, first, 0)

    def sweep(src, dst, j):
        wts = weights(j)
        for g in range(HALF // 8):
            p_re = slice(8 * g, 8 * g + 8)
            p_im = slice(HALF + 8 * g, HALF + 8 * g + 8)
            n_re = near(wts, src[j, p_re, :], src[j - 1, p_re, :], src[j + 1, p_re, :])
            n_im = near(wts, src[j, p_im, :], src[j - 1, p_im, :], src[j + 1, p_im, :])
            a_re, b = a_ref[j, p_re, :], b_ref[j, p_re, :]
            a_im = alt_ref[j] if g == 0 else a_re
            dst[j, p_re, :] = f_ref[j, p_re, :] + (n_re * a_re + n_im * b)
            dst[j, p_im, :] = f_ref[j, p_im, :] + (n_im * a_im - n_re * b)

    src = f_ref
    for m in range(2, SWEEPS + 1):
        dst = w_ref if m % 2 == 0 else v_ref

        def body(j, carry, src=src, dst=dst):
            sweep(src, dst, j)
            return carry

        lax.fori_loop(m, SPAN - m, body, 0)
        src = dst

    for r in range(0, ROWS, 2):
        j = ROWS + r
        pair = jnp.concatenate([src[j, :, :LANES], src[j + 1, :, :LANES]], 1)
        corr = mul(inv_ref[...], pair)
        out_ref[pl.ds(r, STEPS, stride=ROWS), :] = x_ref[j, 8:, :LANES] + corr[:, :LANES]
        out_ref[pl.ds(r + 1, STEPS, stride=ROWS), :] = x_ref[j + 1, 8:, :LANES] + corr[:, LANES:]


def place_kernel(in_ref, out_ref):
    for d in range(DEVS):
        for n in range(LOCAL):
            out_ref[n, :, d * LANES : (d + 1) * LANES] = in_ref[d, n * ROWS : (n + 1) * ROWS, :]


def vmem(count):
    return [pl.BlockSpec(memory_space=pltpu.VMEM)] * count


def pack(t, iterate, initial, diffusion, courant_x, courant_y):
    return pl.pallas_call(
        pack_kernel,
        name="pack",
        out_shape=(
            jax.ShapeDtypeStruct((DEVS, BLOCK, LANES), F32),
            jax.ShapeDtypeStruct((BLOCK, LANES), F32),
        ),
        in_specs=[pl.BlockSpec(memory_space=pltpu.SMEM)] + vmem(5),
        out_specs=tuple(vmem(2)),
    )(t, iterate, initial, diffusion, courant_x, courant_y)


def solve(up, own, down, coef_up, coef, coef_down):
    fwd, inv, shifts = tables()
    big = pltpu.VMEM((SPAN, STEPS, WIDE), F32)
    half = pltpu.VMEM((SPAN, HALF, WIDE), F32)
    return pl.pallas_call(
        solve_kernel,
        name="solve",
        out_shape=jax.ShapeDtypeStruct((STEPS * ROWS, LANES), F32),
        in_specs=vmem(9),
        out_specs=vmem(1)[0],
        scratch_shapes=[
            pltpu.VMEM((SPAN, STEPS + 8, WIDE), F32),
            pltpu.VMEM((STEPS, LANES), F32),
            pltpu.VMEM((LOCAL, ROWS, LANES), F32),
            pltpu.VMEM((5, SPAN, WIDE), F32),
            half,
            pltpu.VMEM((SPAN, 8, WIDE), F32),
            half,
            big,
            big,
            big,
        ],
        compiler_params=pltpu.CompilerParams(vmem_limit_bytes=32 * 1024 * 1024),
    )(jnp.asarray(fwd), jnp.asarray(inv), jnp.asarray(shifts), up, own, down, coef_up, coef, coef_down)


def place(received):
    return pl.pallas_call(
        place_kernel,
        name="place",
        out_shape=jax.ShapeDtypeStruct((LOCAL, ROWS, DEVS * LANES), F32),
        in_specs=vmem(1),
        out_specs=vmem(1)[0],
    )(received)


def local(iterate, initial, diffusion, courant_x, courant_y):
    t = lax.axis_index("tm").astype(jnp.int32).reshape(1)
    send, coef = pack(t, iterate, initial, diffusion, courant_x, courant_y)
    count = lax.axis_size("space")
    down = [(i, i + 1) for i in range(count - 1)]
    up = [(i + 1, i) for i in range(count - 1)]
    coef_up = lax.ppermute(coef, "space", down)
    coef_down = lax.ppermute(coef, "space", up)
    own = lax.all_to_all(send, "tm", split_axis=0, concat_axis=0, tiled=True)
    own = own.reshape(DEVS * BLOCK, LANES)
    above = lax.ppermute(own, "space", down)
    below = lax.ppermute(own, "space", up)
    new = solve(above, own, below, coef_up, coef, coef_down)
    back = lax.all_to_all(new.reshape(DEVS, LOCAL * ROWS, LANES), "tm", split_axis=0, concat_axis=0, tiled=True)
    return place(back)


def solution(mesh):
    return jax.shard_map(
        local,
        mesh=mesh,
        in_specs=(
            P("tm", "space", None),
            P("space", None),
            P("space", None),
            P("space", None),
            P("space", None),
        ),
        out_specs=P("tm", "space", None),
        check_vma=False,
    )
```

```python
import math

import jax
import jax.numpy as jnp
import numpy as np
from jax import lax
from jax.experimental import pallas as pl
from jax.experimental.pallas import tpu as pltpu
from jax.sharding import PartitionSpec as P

SWEEPS = 8
ALPHA = 0.01
STEPS = 64
HALF = STEPS // 2
DEVS = 16
LOCAL = STEPS // DEVS
ROWS = 8
LANES = 128
BLOCK = ROWS * LOCAL + ROWS
SPAN = 3 * ROWS
WIDE = 2 * LANES
F32 = jnp.float32


def tables():
    n = np.arange(STEPS)
    g = ALPHA ** (n / STEPS)
    k = np.arange(HALF)
    ang = 2.0 * np.pi * (np.outer(k, n) % STEPS) / STEPS
    fwd = np.concatenate([np.cos(ang) * g, -np.sin(ang) * g], 0)
    fwd[HALF] = (-1.0) ** n * g
    inv = np.concatenate([2.0 * np.cos(ang), -2.0 * np.sin(ang)], 0).T
    inv[:, 0] = 1.0
    inv[:, HALF] = (-1.0) ** n
    inv = inv / (STEPS * g[:, None])
    beta = ALPHA ** (1.0 / STEPS)
    shift_re = 1.0 - beta * np.cos(2.0 * np.pi * k / STEPS)
    shift_im = beta * np.sin(2.0 * np.pi * k / STEPS)
    shift_alt = shift_re.copy()
    shift_alt[0] = 1.0 + beta
    shifts = np.zeros((HALF, 3 * LANES), np.float32)
    shifts[:, :LANES] = shift_re[:, None]
    shifts[:, LANES : 2 * LANES] = shift_im[:, None]
    shifts[:, 2 * LANES :] = shift_alt[:, None]
    return fwd.astype(np.float32), inv.astype(np.float32), shifts


def lane_ids(rows):
    return lax.broadcasted_iota(jnp.int32, (rows, LANES), 1)


def rim(left, right):
    lane = lane_ids(ROWS)
    both = jnp.where(lane < 8, right, jnp.where(lane >= LANES - 8, left, 0.0))
    moved = pltpu.roll(both, 8, 1, stride=16, stride_axis=0)
    return jnp.sum(moved, axis=0, keepdims=True)


def pack_kernel(t_ref, it_ref, ini_ref, dif_ref, cx_ref, cy_ref, send_ref):
    t = t_ref[0]
    which, share = t % 4, t // 4
    coef = jnp.where(which < 2, jnp.where(which == 0, ini_ref[...], dif_ref[...]), jnp.where(which == 2, cx_ref[...], cy_ref[...]))
    turned = pltpu.roll(coef, (ROWS - 2 * share) % ROWS, 0)
    zero = jnp.zeros((ROWS, LANES), F32)

    def sides(cols, d):
        return rim(cols(d - 1) if d else zero, cols(d + 1) if d + 1 < DEVS else zero)

    for d in range(DEVS):
        rims = []
        for n in range(LOCAL):
            cols = lambda e: it_ref[n, :, e * LANES : (e + 1) * LANES]
            send_ref[d, n * ROWS : (n + 1) * ROWS, :] = cols(d)
            rims.append(sides(cols, d))
        rims.append(turned[:2, d * LANES : (d + 1) * LANES])
        rims.append(sides(lambda e: coef[:, e * LANES : (e + 1) * LANES], d))
        rims.append(jnp.zeros((1, LANES), F32))
        send_ref[d, LOCAL * ROWS :, :] = jnp.concatenate(rims, 0)


def mul(matrix, value):
    return jnp.dot(matrix, value, precision=lax.Precision.HIGHEST, preferred_element_type=F32)


def solve_kernel(
    fwd_ref, inv_ref, shift_ref, up_ref, own_ref, dn_ref,
    out_ref, x_ref, rim_ref, coef_ref, wt_ref, a_ref, alt_ref, b_ref, f_ref, w_ref, v_ref,
):
    lane = lane_ids(1)
    inside = (lane < 8) | (lane >= LANES - 8)
    for blk, ref in enumerate((up_ref, own_ref, dn_ref)):
        for d in range(DEVS):
            base = d * BLOCK + LOCAL * ROWS
            rim_ref[d * LOCAL : (d + 1) * LOCAL, :] = ref[base : base + LOCAL, :]
            share = 2 * (d // 4)
            coef_ref[d % 4, share : share + 2, :LANES] = ref[base + LOCAL : base + LOCAL + 2, :]
            if d < 4:
                rim_ref[STEPS + d : STEPS + d + 1, :] = ref[base + LOCAL + 2 : base + LOCAL + 3, :]
        rims = rim_ref[...]
        for r in range(ROWS):
            j = blk * ROWS + r
            for d in range(DEVS):
                x_ref[j, 8 + d * LOCAL : 8 + (d + 1) * LOCAL, :LANES] = ref[pl.ds(d * BLOCK + r, LOCAL, stride=ROWS), :]
            turned = jnp.where(inside, pltpu.roll(rims, (2 * LANES - 16 * r - 8) % LANES, 1), 0.0)
            x_ref[j, 8:, LANES:] = turned[:STEPS]
            for a in range(4):
                coef_ref[a, r : r + 1, LANES:] = turned[STEPS + a : STEPS + a + 1]
            x_ref[j, 7:8, :] = coef_ref[0, r : r + 1, :]
        dif, cx, cy = coef_ref[1], coef_ref[2], coef_ref[3]
        west = dif + jnp.maximum(cx, 0.0)
        east = dif + jnp.maximum(-cx, 0.0)
        north = dif + jnp.maximum(cy, 0.0)
        south = dif + jnp.maximum(-cy, 0.0)
        rows = slice(blk * ROWS, (blk + 1) * ROWS)
        for a, value in enumerate((west, east, north, south, west + east + north + south)):
            wt_ref[a, rows, :] = value

    def weights(j):
        return [wt_ref[a, j : j + 1, :] for a in range(5)]

    def near(wts, here, above, below):
        summed = wts[0] * pltpu.roll(here, 1, 1) + wts[1] * pltpu.roll(here, WIDE - 1, 1)
        return summed + wts[2] * above + wts[3] * below

    def first(j):
        wts = weights(j)
        here = x_ref[j, 8:, :]
        r = x_ref[j, 7 : 7 + STEPS, :] - here + near(wts, here, x_ref[j - 1, 8:, :], x_ref[j + 1, 8:, :]) - wts[4] * here
        hat = mul(fwd_ref[...], r)
        for g in range(HALF // 8):
            part = slice(8 * g, 8 * g + 8)
            h_re, h_im = hat[8 * g : 8 * g + 8], hat[HALF + 8 * g : HALF + 8 * g + 8]
            rep = lambda c: jnp.concatenate([shift_ref[part, c * LANES : (c + 1) * LANES]] * 2, 1)
            s_im = rep(1)
            d_re = rep(0) + wts[4]
            norm = 1.0 / (d_re * d_re + s_im * s_im)
            a_re = d_re * norm
            a_im = a_re
            b = s_im * norm
            if g == 0:
                d_im = rep(2) + wts[4]
                a_im = d_im * (1.0 / (d_im * d_im + s_im * s_im))
                alt_ref[j] = a_im
            a_ref[j, part, :] = a_re
            b_ref[j, part, :] = b
            w_re = h_re * a_re + h_im * b
            w_im = h_im * a_im - h_re * b
            f_ref[j, part, :] = w_re
            f_ref[j, HALF + 8 * g : HALF + 8 * g + 8, :] = w_im

    for j in range(1, SPAN - 1):
        first(j)

    def sweep(src, dst, j):
        wts = weights(j)
        for g in range(HALF // 8):
            p_re = slice(8 * g, 8 * g + 8)
            p_im = slice(HALF + 8 * g, HALF + 8 * g + 8)
            n_re = near(wts, src[j, p_re, :], src[j - 1, p_re, :], src[j + 1, p_re, :])
            n_im = near(wts, src[j, p_im, :], src[j - 1, p_im, :], src[j + 1, p_im, :])
            a_re, b = a_ref[j, p_re, :], b_ref[j, p_re, :]
            a_im = alt_ref[j] if g == 0 else a_re
            dst[j, p_re, :] = f_ref[j, p_re, :] + (n_re * a_re + n_im * b)
            dst[j, p_im, :] = f_ref[j, p_im, :] + (n_im * a_im - n_re * b)

    src = f_ref
    for m in range(2, SWEEPS + 1):
        dst = w_ref if m % 2 == 0 else v_ref
        for j in range(m, SPAN - m):
            sweep(src, dst, j)
        src = dst

    for r in range(0, ROWS, 2):
        j = ROWS + r
        pair = jnp.concatenate([src[j, :, :LANES], src[j + 1, :, :LANES]], 1)
        corr = mul(inv_ref[...], pair)
        out_ref[pl.ds(r, STEPS, stride=ROWS), :] = x_ref[j, 8:, :LANES] + corr[:, :LANES]
        out_ref[pl.ds(r + 1, STEPS, stride=ROWS), :] = x_ref[j + 1, 8:, :LANES] + corr[:, LANES:]


def place_kernel(in_ref, out_ref):
    for d in range(DEVS):
        for n in range(LOCAL):
            out_ref[n, :, d * LANES : (d + 1) * LANES] = in_ref[d, n * ROWS : (n + 1) * ROWS, :]


def vmem(count):
    return [pl.BlockSpec(memory_space=pltpu.VMEM)] * count


def pack(t, iterate, initial, diffusion, courant_x, courant_y):
    return pl.pallas_call(
        pack_kernel,
        name="pack",
        out_shape=jax.ShapeDtypeStruct((DEVS, BLOCK, LANES), F32),
        in_specs=[pl.BlockSpec(memory_space=pltpu.SMEM)] + vmem(5),
        out_specs=vmem(1)[0],
    )(t, iterate, initial, diffusion, courant_x, courant_y)


def solve(up, own, down):
    fwd, inv, shifts = tables()
    big = pltpu.VMEM((SPAN, STEPS, WIDE), F32)
    half = pltpu.VMEM((SPAN, HALF, WIDE), F32)
    return pl.pallas_call(
        solve_kernel,
        name="solve",
        out_shape=jax.ShapeDtypeStruct((STEPS * ROWS, LANES), F32),
        in_specs=vmem(6),
        out_specs=vmem(1)[0],
        scratch_shapes=[
            pltpu.VMEM((SPAN, STEPS + 8, WIDE), F32),
            pltpu.VMEM((STEPS + 8, LANES), F32),
            pltpu.VMEM((4, ROWS, WIDE), F32),
            pltpu.VMEM((5, SPAN, WIDE), F32),
            half,
            pltpu.VMEM((SPAN, 8, WIDE), F32),
            half,
            big,
            big,
            big,
        ],
        compiler_params=pltpu.CompilerParams(vmem_limit_bytes=32 * 1024 * 1024),
    )(jnp.asarray(fwd), jnp.asarray(inv), jnp.asarray(shifts), up, own, down)


def place(received):
    return pl.pallas_call(
        place_kernel,
        name="place",
        out_shape=jax.ShapeDtypeStruct((LOCAL, ROWS, DEVS * LANES), F32),
        in_specs=vmem(1),
        out_specs=vmem(1)[0],
    )(received)


def local(iterate, initial, diffusion, courant_x, courant_y):
    t = lax.axis_index("tm").astype(jnp.int32).reshape(1)
    send = pack(t, iterate, initial, diffusion, courant_x, courant_y)
    count = lax.axis_size("space")
    down = [(i, i + 1) for i in range(count - 1)]
    up = [(i + 1, i) for i in range(count - 1)]
    own = lax.all_to_all(send, "tm", split_axis=0, concat_axis=0, tiled=True)
    own = own.reshape(DEVS * BLOCK, LANES)
    above = lax.ppermute(own, "space", down)
    below = lax.ppermute(own, "space", up)
    new = solve(above, own, below)
    back = lax.all_to_all(new.reshape(DEVS, LOCAL * ROWS, LANES), "tm", split_axis=0, concat_axis=0, tiled=True)
    return place(back)


def solution(mesh):
    return jax.shard_map(
        local,
        mesh=mesh,
        in_specs=(
            P("tm", "space", None),
            P("space", None),
            P("space", None),
            P("space", None),
            P("space", None),
        ),
        out_specs=P("tm", "space", None),
        check_vma=False,
    )
```

```python
import math

import jax
import jax.numpy as jnp
import numpy as np
from jax import lax
from jax.experimental import pallas as pl
from jax.experimental.pallas import tpu as pltpu
from jax.sharding import PartitionSpec as P

SWEEPS = 8
ALPHA = 0.01
STEPS = 64
HALF = STEPS // 2
DEVS = 16
LOCAL = STEPS // DEVS
ROWS = 8
LANES = 128
BLOCK = ROWS * LOCAL + ROWS
SPAN = 3 * ROWS
WIDE = 2 * LANES
F32 = jnp.float32


def tables():
    n = np.arange(STEPS)
    g = ALPHA ** (n / STEPS)
    k = np.arange(HALF)
    ang = 2.0 * np.pi * (np.outer(k, n) % STEPS) / STEPS
    fwd = np.concatenate([np.cos(ang) * g, -np.sin(ang) * g], 0)
    fwd[HALF] = (-1.0) ** n * g
    inv = np.concatenate([2.0 * np.cos(ang), -2.0 * np.sin(ang)], 0).T
    inv[:, 0] = 1.0
    inv[:, HALF] = (-1.0) ** n
    inv = inv / (STEPS * g[:, None])
    beta = ALPHA ** (1.0 / STEPS)
    shift_re = 1.0 - beta * np.cos(2.0 * np.pi * k / STEPS)
    shift_im = beta * np.sin(2.0 * np.pi * k / STEPS)
    shift_alt = shift_re.copy()
    shift_alt[0] = 1.0 + beta
    shifts = np.zeros((HALF, 3 * LANES), np.float32)
    shifts[:, :LANES] = shift_re[:, None]
    shifts[:, LANES : 2 * LANES] = shift_im[:, None]
    shifts[:, 2 * LANES :] = shift_alt[:, None]
    return fwd.astype(np.float32), inv.astype(np.float32), shifts


def lane_ids(rows):
    return lax.broadcasted_iota(jnp.int32, (rows, LANES), 1)


def rim(left, right):
    lane = lane_ids(ROWS)
    both = jnp.where(lane < 8, right, jnp.where(lane >= LANES - 8, left, 0.0))
    moved = pltpu.roll(both, 8, 1, stride=16, stride_axis=0)
    return jnp.sum(moved, axis=0, keepdims=True)


def pack_kernel(t_ref, it_ref, ini_ref, dif_ref, cx_ref, cy_ref, send_ref):
    t = t_ref[0]
    which, share = t % 4, t // 4
    coef = jnp.where(which < 2, jnp.where(which == 0, ini_ref[...], dif_ref[...]), jnp.where(which == 2, cx_ref[...], cy_ref[...]))
    turned = pltpu.roll(coef, (ROWS - 2 * share) % ROWS, 0)
    zero = jnp.zeros((ROWS, LANES), F32)

    def sides(cols, d):
        return rim(cols(d - 1) if d else zero, cols(d + 1) if d + 1 < DEVS else zero)

    for d in range(DEVS):
        rims = []
        for n in range(LOCAL):
            cols = lambda e: it_ref[n, :, e * LANES : (e + 1) * LANES]
            send_ref[d, n * ROWS : (n + 1) * ROWS, :] = cols(d)
            rims.append(sides(cols, d))
        rims.append(turned[:2, d * LANES : (d + 1) * LANES])
        rims.append(sides(lambda e: coef[:, e * LANES : (e + 1) * LANES], d))
        rims.append(jnp.zeros((1, LANES), F32))
        send_ref[d, LOCAL * ROWS :, :] = jnp.concatenate(rims, 0)


def mul(matrix, value):
    return jnp.dot(matrix, value, precision=lax.Precision.HIGHEST, preferred_element_type=F32)


def row(refs, j):
    return refs[j // ROWS].at[j % ROWS]


def build(ref, x_ref, wt_ref, rim_ref, coef_ref):
    lane = lane_ids(1)
    inside = (lane < 8) | (lane >= LANES - 8)
    for d in range(DEVS):
        base = d * BLOCK + LOCAL * ROWS
        rim_ref[d * LOCAL : (d + 1) * LOCAL, :] = ref[base : base + LOCAL, :]
        share = 2 * (d // 4)
        coef_ref[d % 4, share : share + 2, :LANES] = ref[base + LOCAL : base + LOCAL + 2, :]
        if d < 4:
            rim_ref[STEPS + d : STEPS + d + 1, :] = ref[base + LOCAL + 2 : base + LOCAL + 3, :]
    rims = rim_ref[...]
    for r in range(ROWS):
        for d in range(DEVS):
            x_ref[r, 8 + d * LOCAL : 8 + (d + 1) * LOCAL, :LANES] = ref[pl.ds(d * BLOCK + r, LOCAL, stride=ROWS), :]
        turned = jnp.where(inside, pltpu.roll(rims, (2 * LANES - 16 * r - 8) % LANES, 1), 0.0)
        x_ref[r, 8:, LANES:] = turned[:STEPS]
        for a in range(4):
            coef_ref[a, r : r + 1, LANES:] = turned[STEPS + a : STEPS + a + 1]
        x_ref[r, 7:8, :] = coef_ref[0, r : r + 1, :]
    dif, cx, cy = coef_ref[1], coef_ref[2], coef_ref[3]
    west = dif + jnp.maximum(cx, 0.0)
    east = dif + jnp.maximum(-cx, 0.0)
    north = dif + jnp.maximum(cy, 0.0)
    south = dif + jnp.maximum(-cy, 0.0)
    for a, value in enumerate((west, east, north, south, west + east + north + south)):
        wt_ref[a] = value


def diagonal(shift_ref, wt_ref, a_ref, alt_ref, b_ref, r):
    centre = wt_ref[4, r : r + 1, :]
    for g in range(HALF // 8):
        part = slice(8 * g, 8 * g + 8)
        rep = lambda c: jnp.concatenate([shift_ref[part, c * LANES : (c + 1) * LANES]] * 2, 1)
        s_im = rep(1)
        d_re = rep(0) + centre
        norm = 1.0 / (d_re * d_re + s_im * s_im)
        a_ref[r, part, :] = d_re * norm
        b_ref[r, part, :] = s_im * norm
        if g == 0:
            d_im = rep(2) + centre
            alt_ref[r] = d_im * (1.0 / (d_im * d_im + s_im * s_im))


def near(wts, here, above, below):
    width = here.shape[1]
    summed = wts[0] * pltpu.roll(here, 1, 1) + wts[1] * pltpu.roll(here, width - 1, 1)
    return summed + wts[2] * above + wts[3] * below


class Grid:
    def __init__(self, x, wt, a, alt, b):
        self.x, self.wt, self.a, self.alt, self.b = x, wt, a, alt, b

    def weights(self, j):
        ref, r = self.wt[j // ROWS], j % ROWS
        return [ref[a, r : r + 1, :] for a in range(5)]

    def divide(self, j, g, q_re, q_im):
        part = slice(8 * g, 8 * g + 8)
        cols = slice(0, q_re.shape[1])
        a_re, b = row(self.a, j)[part, cols], row(self.b, j)[part, cols]
        a_im = row(self.alt, j)[:, cols] if g == 0 else a_re
        return q_re * a_re + q_im * b, q_im * a_im - q_re * b

    def first(self, fwd_ref, j, dst):
        wts = self.weights(j)
        here = row(self.x, j)[8:, :]
        r = row(self.x, j)[7 : 7 + STEPS, :] - here
        r = r + near(wts, here, row(self.x, j - 1)[8:, :], row(self.x, j + 1)[8:, :]) - wts[4] * here
        hat = mul(fwd_ref[...], r)
        for g in range(HALF // 8):
            p_re, p_im = parts(g)
            dst[p_re, :], dst[p_im, :] = self.divide(j, g, hat[p_re], hat[p_im])

    def sweep(self, j, level, last):
        m, width = last, LANES if last == SWEEPS else WIDE
        wts = self.weights(j)
        here, above, below = level(m - 1, j), level(m - 1, j - 1), level(m - 1, j + 1)
        base, dst = level(1, j), level(m, j)
        for g in range(HALF // 8):
            sums = [near(wts, here[p, :], above[p, :], below[p, :])[:, :width] for p in parts(g)]
            for p, value in zip(parts(g), self.divide(j, g, *sums)):
                dst[p, :width] = base[p, :width] + value


def parts(g):
    return slice(8 * g, 8 * g + 8), slice(HALF + 8 * g, HALF + 8 * g + 8)


def own_kernel(fwd_ref, shift_ref, own_ref, x_ref, wt_ref, a_ref, alt_ref, b_ref, f_ref, rim_ref, coef_ref):
    build(own_ref, x_ref, wt_ref, rim_ref, coef_ref)
    grid = Grid(*[(None, ref, None) for ref in (x_ref, wt_ref, a_ref, alt_ref, b_ref)])
    for r in range(ROWS):
        diagonal(shift_ref, wt_ref, a_ref, alt_ref, b_ref, r)
    for r in range(1, ROWS - 1):
        grid.first(fwd_ref, ROWS + r, f_ref.at[r])


def below_kernel(
    fwd_ref, shift_ref, dn_ref, x1, wt1, a1, alt1, b1, f1,
    f15_ref, edge_ref, x_ref, wt_ref, a_ref, alt_ref, b_ref, f_ref, w_ref, rim_ref, coef_ref,
):
    build(dn_ref, x_ref, wt_ref, rim_ref, coef_ref)
    grid = Grid((None, x1, x_ref), (None, wt1, wt_ref), (None, a1, a_ref), (None, alt1, alt_ref), (None, b1, b_ref))
    for r in range(ROWS - 1):
        diagonal(shift_ref, wt_ref, a_ref, alt_ref, b_ref, r)

    def level(m, j):
        if m == 1:
            return f1.at[j - 8] if j < 15 else f15_ref if j == 15 else f_ref.at[j - 16]
        return edge_ref.at[m - 2, j - 8 - m] if j <= 9 + m else w_ref.at[m % 2, j - 8]

    for j in range(15, SPAN - 1):
        grid.first(fwd_ref, j, level(1, j))
    for m in range(2, SWEEPS):
        for j in range(8 + m, SPAN - m):
            grid.sweep(j, level, m)


def last_kernel(
    fwd_ref, inv_ref, shift_ref, up_ref, x1, wt1, a1, alt1, b1, f1, f15_ref, edge_ref,
    out_ref, x_ref, wt_ref, a_ref, alt_ref, b_ref, f_ref, w_ref, rim_ref, coef_ref,
):
    build(up_ref, x_ref, wt_ref, rim_ref, coef_ref)
    grid = Grid((x_ref, x1), (wt_ref, wt1), (a_ref, a1), (alt_ref, alt1), (b_ref, b1))
    for r in range(1, ROWS):
        diagonal(shift_ref, wt_ref, a_ref, alt_ref, b_ref, r)

    def level(m, j):
        if m == 1:
            return f_ref.at[j] if j <= 8 else f1.at[j - 8] if j < 15 else f15_ref
        return w_ref.at[m % 2, j] if j <= 7 + m else edge_ref.at[m - 2, j - 8 - m]

    for j in range(1, ROWS + 1):
        grid.first(fwd_ref, j, level(1, j))
    for m in range(2, SWEEPS + 1):
        for j in range(m, 8 + m):
            grid.sweep(j, level, m)

    for r in range(0, ROWS, 2):
        j = ROWS + r
        pair = jnp.concatenate([level(SWEEPS, j)[:, :LANES], level(SWEEPS, j + 1)[:, :LANES]], 1)
        corr = mul(inv_ref[...], pair)
        out_ref[pl.ds(r, STEPS, stride=ROWS), :] = x1[r, 8:, :LANES] + corr[:, :LANES]
        out_ref[pl.ds(r + 1, STEPS, stride=ROWS), :] = x1[r + 1, 8:, :LANES] + corr[:, LANES:]


def place_kernel(in_ref, out_ref):
    for d in range(DEVS):
        for n in range(LOCAL):
            out_ref[n, :, d * LANES : (d + 1) * LANES] = in_ref[d, n * ROWS : (n + 1) * ROWS, :]


def vmem(count):
    return [pl.BlockSpec(memory_space=pltpu.VMEM)] * count


def pack(t, iterate, initial, diffusion, courant_x, courant_y):
    return pl.pallas_call(
        pack_kernel,
        name="pack",
        out_shape=jax.ShapeDtypeStruct((DEVS, BLOCK, LANES), F32),
        in_specs=[pl.BlockSpec(memory_space=pltpu.SMEM)] + vmem(5),
        out_specs=vmem(1)[0],
    )(t, iterate, initial, diffusion, courant_x, courant_y)


BLOCKS = {
    "x": (ROWS, STEPS + 8, WIDE),
    "wt": (5, ROWS, WIDE),
    "a": (ROWS, HALF, WIDE),
    "alt": (ROWS, 8, WIDE),
    "b": (ROWS, HALF, WIDE),
}
FIELDS = (ROWS, STEPS, WIDE)
PAIRS = (SWEEPS - 2, 2, STEPS, WIDE)
EXTRA = [pltpu.VMEM((STEPS + 8, LANES), F32), pltpu.VMEM((4, ROWS, WIDE), F32)]


def call(kernel, name, flops, operands, shapes, scratch):
    return pl.pallas_call(
        kernel,
        name=name,
        out_shape=tuple(jax.ShapeDtypeStruct(shape, F32) for shape in shapes),
        in_specs=vmem(len(operands)),
        out_specs=tuple(vmem(len(shapes))),
        scratch_shapes=[pltpu.VMEM(shape, F32) for shape in scratch] + EXTRA,
        compiler_params=pltpu.CompilerParams(vmem_limit_bytes=24 * 1024 * 1024),
        cost_estimate=pl.CostEstimate(flops=flops, bytes_accessed=2**20, transcendentals=0),
    )(*operands)


def solve(up, own, down):
    fwd, inv, shifts = [jnp.asarray(table) for table in tables()]
    block = list(BLOCKS.values())
    mine = call(own_kernel, "own", 10**7, (fwd, shifts, own), block + [FIELDS], [])
    low = call(below_kernel, "below", 2 * 10**7, (fwd, shifts, down) + tuple(mine), [(STEPS, WIDE), PAIRS], block + [FIELDS, (2, 2 * ROWS, STEPS, WIDE)])
    args = (fwd, inv, shifts, up) + tuple(mine) + tuple(low)
    return call(last_kernel, "last", 3 * 10**7, args, [(STEPS * ROWS, LANES)], block + [(ROWS + 1, STEPS, WIDE), (2, 2 * ROWS, STEPS, WIDE)])[0]


def place(received):
    return pl.pallas_call(
        place_kernel,
        name="place",
        out_shape=jax.ShapeDtypeStruct((LOCAL, ROWS, DEVS * LANES), F32),
        in_specs=vmem(1),
        out_specs=vmem(1)[0],
    )(received)


def local(iterate, initial, diffusion, courant_x, courant_y):
    t = lax.axis_index("tm").astype(jnp.int32).reshape(1)
    send = pack(t, iterate, initial, diffusion, courant_x, courant_y)
    count = lax.axis_size("space")
    down = [(i, i + 1) for i in range(count - 1)]
    up = [(i + 1, i) for i in range(count - 1)]
    own = lax.all_to_all(send, "tm", split_axis=0, concat_axis=0, tiled=True)
    own = own.reshape(DEVS * BLOCK, LANES)
    above = lax.ppermute(own, "space", down)
    below = lax.ppermute(own, "space", up)
    new = solve(above, own, below)
    back = lax.all_to_all(new.reshape(DEVS, LOCAL * ROWS, LANES), "tm", split_axis=0, concat_axis=0, tiled=True)
    return place(back)


def solution(mesh):
    return jax.shard_map(
        local,
        mesh=mesh,
        in_specs=(
            P("tm", "space", None),
            P("space", None),
            P("space", None),
            P("space", None),
            P("space", None),
        ),
        out_specs=P("tm", "space", None),
        check_vma=False,
    )
```

```python
import math

import jax
import jax.numpy as jnp
import numpy as np
from jax import lax
from jax.experimental import pallas as pl
from jax.experimental.pallas import tpu as pltpu
from jax.sharding import PartitionSpec as P

SWEEPS = 8
ALPHA = 0.01
STEPS = 64
HALF = STEPS // 2
DEVS = 16
LOCAL = STEPS // DEVS
ROWS = 8
LANES = 128
BLOCK = ROWS * LOCAL + ROWS
SPAN = 3 * ROWS
WIDE = 2 * LANES
F32 = jnp.float32


def tables():
    n = np.arange(STEPS)
    g = ALPHA ** (n / STEPS)
    k = np.arange(HALF)
    ang = 2.0 * np.pi * (np.outer(k, n) % STEPS) / STEPS
    fwd = np.concatenate([np.cos(ang) * g, -np.sin(ang) * g], 0)
    fwd[HALF] = (-1.0) ** n * g
    inv = np.concatenate([2.0 * np.cos(ang), -2.0 * np.sin(ang)], 0).T
    inv[:, 0] = 1.0
    inv[:, HALF] = (-1.0) ** n
    inv = inv / (STEPS * g[:, None])
    beta = ALPHA ** (1.0 / STEPS)
    shift_re = 1.0 - beta * np.cos(2.0 * np.pi * k / STEPS)
    shift_im = beta * np.sin(2.0 * np.pi * k / STEPS)
    shift_alt = shift_re.copy()
    shift_alt[0] = 1.0 + beta
    shifts = np.zeros((HALF, 3 * LANES), np.float32)
    shifts[:, :LANES] = shift_re[:, None]
    shifts[:, LANES : 2 * LANES] = shift_im[:, None]
    shifts[:, 2 * LANES :] = shift_alt[:, None]
    return fwd.astype(np.float32), inv.astype(np.float32), shifts


def lane_ids(rows):
    return lax.broadcasted_iota(jnp.int32, (rows, LANES), 1)


def rim(left, right):
    lane = lane_ids(ROWS)
    both = jnp.where(lane < 8, right, jnp.where(lane >= LANES - 8, left, 0.0))
    moved = pltpu.roll(both, 8, 1, stride=16, stride_axis=0)
    return jnp.sum(moved, axis=0, keepdims=True)


def pack_kernel(t_ref, it_ref, ini_ref, dif_ref, cx_ref, cy_ref, send_ref):
    t = t_ref[0]
    which, share = t % 4, t // 4
    coef = jnp.where(which < 2, jnp.where(which == 0, ini_ref[...], dif_ref[...]), jnp.where(which == 2, cx_ref[...], cy_ref[...]))
    turned = pltpu.roll(coef, (ROWS - 2 * share) % ROWS, 0)
    zero = jnp.zeros((ROWS, LANES), F32)

    def sides(cols, d):
        return rim(cols(d - 1) if d else zero, cols(d + 1) if d + 1 < DEVS else zero)

    for d in range(DEVS):
        rims = []
        for n in range(LOCAL):
            cols = lambda e: it_ref[n, :, e * LANES : (e + 1) * LANES]
            send_ref[d, n * ROWS : (n + 1) * ROWS, :] = cols(d)
            rims.append(sides(cols, d))
        rims.append(turned[:2, d * LANES : (d + 1) * LANES])
        rims.append(sides(lambda e: coef[:, e * LANES : (e + 1) * LANES], d))
        rims.append(jnp.zeros((1, LANES), F32))
        send_ref[d, LOCAL * ROWS :, :] = jnp.concatenate(rims, 0)


def mul(matrix, value):
    return jnp.dot(matrix, value, precision=lax.Precision.HIGHEST, preferred_element_type=F32)


def row(refs, j):
    return refs[j // ROWS].at[j % ROWS]


def build(ref, x_ref, wt_ref, rim_ref, coef_ref, main_ref=None):
    def tiles(main, turned):
        lane = lane_ids(main.shape[0])
        return jnp.where(lane >= LANES - 8, turned, main), jnp.where(lane < 8, turned, main)

    for d in range(DEVS):
        base = d * BLOCK + LOCAL * ROWS
        rim_ref[d * LOCAL : (d + 1) * LOCAL, :] = ref[base : base + LOCAL, :]
        share = 2 * (d // 4)
        coef_ref[d % 4, share : share + 2, :LANES] = ref[base + LOCAL : base + LOCAL + 2, :]
        if d < 4:
            rim_ref[STEPS + d : STEPS + d + 1, :] = ref[base + LOCAL + 2 : base + LOCAL + 3, :]
    rims = rim_ref[...]
    for r in range(ROWS):
        for d in range(DEVS):
            x_ref[r, 8 + d * LOCAL : 8 + (d + 1) * LOCAL, :LANES] = ref[pl.ds(d * BLOCK + r, LOCAL, stride=ROWS), :]
        turned = pltpu.roll(rims, (2 * LANES - 16 * r - 8) % LANES, 1)
        main = x_ref[r, 8:, :LANES]
        if main_ref is not None:
            main_ref[r] = main
        x_ref[r, 8:, :LANES], x_ref[r, 8:, LANES:] = tiles(main, turned[:STEPS])
        for a in range(4):
            one = slice(r, r + 1)
            coef_ref[a, one, :LANES], coef_ref[a, one, LANES:] = tiles(coef_ref[a, one, :LANES], turned[STEPS + a : STEPS + a + 1])
        x_ref[r, 7:8, :] = coef_ref[0, r : r + 1, :]
    dif, cx, cy = coef_ref[1], coef_ref[2], coef_ref[3]
    west = dif + jnp.maximum(cx, 0.0)
    east = dif + jnp.maximum(-cx, 0.0)
    north = dif + jnp.maximum(cy, 0.0)
    south = dif + jnp.maximum(-cy, 0.0)
    for a, value in enumerate((west, east, north, south, west + east + north + south)):
        wt_ref[a] = value


def diagonal(shift_ref, wt_ref, a_ref, alt_ref, b_ref, r):
    centre = wt_ref[4, r : r + 1, :]
    for g in range(HALF // 8):
        part = slice(8 * g, 8 * g + 8)
        rep = lambda c: jnp.concatenate([shift_ref[part, c * LANES : (c + 1) * LANES]] * 2, 1)
        s_im = rep(1)
        d_re = rep(0) + centre
        norm = 1.0 / (d_re * d_re + s_im * s_im)
        a_ref[r, part, :] = d_re * norm
        b_ref[r, part, :] = s_im * norm
        if g == 0:
            d_im = rep(2) + centre
            alt_ref[r] = d_im * (1.0 / (d_im * d_im + s_im * s_im))


def near(wts, here, above, below):
    west, east = [
        jnp.concatenate([pltpu.roll(here[:, :LANES], by, 1), pltpu.roll(here[:, LANES:], by, 1)], 1) for by in (1, LANES - 1)
    ]
    summed = wts[0] * west + wts[1] * east
    return summed + wts[2] * above + wts[3] * below


class Grid:
    def __init__(self, x, wt, a, alt, b):
        self.x, self.wt, self.a, self.alt, self.b = x, wt, a, alt, b

    def weights(self, j):
        ref, r = self.wt[j // ROWS], j % ROWS
        return [ref[a, r : r + 1, :] for a in range(5)]

    def divide(self, j, g, q_re, q_im):
        part = slice(8 * g, 8 * g + 8)
        a_re, b = row(self.a, j)[part, :], row(self.b, j)[part, :]
        a_im = row(self.alt, j)[...] if g == 0 else a_re
        return q_re * a_re + q_im * b, q_im * a_im - q_re * b

    def first(self, fwd_ref, j, dst):
        wts = self.weights(j)
        here = row(self.x, j)[8:, :]
        r = row(self.x, j)[7 : 7 + STEPS, :] - here
        r = r + near(wts, here, row(self.x, j - 1)[8:, :], row(self.x, j + 1)[8:, :]) - wts[4] * here
        hat = mul(fwd_ref[...], r)
        for g in range(HALF // 8):
            p_re, p_im = parts(g)
            dst[p_re, :], dst[p_im, :] = self.divide(j, g, hat[p_re], hat[p_im])

    def sweep(self, j, level, m):
        values = {}
        wts = self.weights(j)
        here, above, below = level(m - 1, j), level(m - 1, j - 1), level(m - 1, j + 1)
        base = level(1, j)
        for g in range(HALF // 8):
            sums = [near(wts, here[p, :], above[p, :], below[p, :]) for p in parts(g)]
            for p, value in zip(parts(g), self.divide(j, g, *sums)):
                values[p.start] = base[p, :] + value
        return values

    def store(self, j, level, m):
        dst = level(m, j)
        for start, value in self.sweep(j, level, m).items():
            dst[start : start + 8, :] = value


def parts(g):
    return slice(8 * g, 8 * g + 8), slice(HALF + 8 * g, HALF + 8 * g + 8)


def own_kernel(fwd_ref, shift_ref, own_ref, main_ref, x_ref, wt_ref, a_ref, alt_ref, b_ref, f_ref, rim_ref, coef_ref):
    build(own_ref, x_ref, wt_ref, rim_ref, coef_ref, main_ref)
    grid = Grid(*[(None, ref, None) for ref in (x_ref, wt_ref, a_ref, alt_ref, b_ref)])
    for r in range(ROWS):
        diagonal(shift_ref, wt_ref, a_ref, alt_ref, b_ref, r)
    for r in range(1, ROWS - 1):
        grid.first(fwd_ref, ROWS + r, f_ref.at[r])


def below_kernel(
    fwd_ref, shift_ref, dn_ref, x1, wt1, a1, alt1, b1, f1,
    f15_ref, edge_ref, x_ref, wt_ref, a_ref, alt_ref, b_ref, f_ref, w_ref, rim_ref, coef_ref,
):
    build(dn_ref, x_ref, wt_ref, rim_ref, coef_ref)
    grid = Grid((None, x1, x_ref), (None, wt1, wt_ref), (None, a1, a_ref), (None, alt1, alt_ref), (None, b1, b_ref))
    for r in range(ROWS - 1):
        diagonal(shift_ref, wt_ref, a_ref, alt_ref, b_ref, r)

    def level(m, j):
        if m == 1:
            return f1.at[j - 8] if j < 15 else f15_ref if j == 15 else f_ref.at[j - 16]
        return edge_ref.at[m - 2, j - 8 - m] if j <= 9 + m else w_ref.at[m % 2, j - 8]

    for j in range(15, SPAN - 1):
        grid.first(fwd_ref, j, level(1, j))
    for m in range(2, SWEEPS):
        for j in range(8 + m, SPAN - m):
            grid.store(j, level, m)


def last_kernel(
    fwd_ref, inv_ref, shift_ref, up_ref, main_ref, x1, wt1, a1, alt1, b1, f1, f15_ref, edge_ref,
    out_ref, x_ref, wt_ref, a_ref, alt_ref, b_ref, f_ref, w_ref, rim_ref, coef_ref,
):
    build(up_ref, x_ref, wt_ref, rim_ref, coef_ref)
    grid = Grid((x_ref, x1), (wt_ref, wt1), (a_ref, a1), (alt_ref, alt1), (b_ref, b1))
    for r in range(1, ROWS):
        diagonal(shift_ref, wt_ref, a_ref, alt_ref, b_ref, r)

    def level(m, j):
        if m == 1:
            return f_ref.at[j] if j <= 8 else f1.at[j - 8] if j < 15 else f15_ref
        return w_ref.at[m % 2, j] if j <= 7 + m else edge_ref.at[m - 2, j - 8 - m]

    for j in range(1, ROWS + 1):
        grid.first(fwd_ref, j, level(1, j))
    for m in range(2, SWEEPS):
        for j in range(m, 8 + m):
            grid.store(j, level, m)
    left = lane_ids(8) < LANES // 2

    def final(j):
        values = grid.sweep(j, level, SWEEPS)
        return jnp.concatenate([jnp.where(left, values[p][:, :LANES], values[p][:, LANES:]) for p in range(0, STEPS, 8)], 0)

    for r in range(0, ROWS, 2):
        corr = mul(inv_ref[...], jnp.concatenate([final(ROWS + r), final(ROWS + r + 1)], 1))
        for i in range(2):
            out_ref[pl.ds(r + i, STEPS, stride=ROWS), :] = main_ref[r + i] + corr[:, i * LANES : (i + 1) * LANES]


def vmem(count):
    return [pl.BlockSpec(memory_space=pltpu.VMEM)] * count


def pack(t, iterate, initial, diffusion, courant_x, courant_y):
    return pl.pallas_call(
        pack_kernel,
        name="pack",
        out_shape=jax.ShapeDtypeStruct((DEVS, BLOCK, LANES), F32),
        in_specs=[pl.BlockSpec(memory_space=pltpu.SMEM)] + vmem(5),
        out_specs=vmem(1)[0],
    )(t, iterate, initial, diffusion, courant_x, courant_y)


BLOCKS = {
    "x": (ROWS, STEPS + 8, WIDE),
    "wt": (5, ROWS, WIDE),
    "a": (ROWS, HALF, WIDE),
    "alt": (ROWS, 8, WIDE),
    "b": (ROWS, HALF, WIDE),
}
FIELDS = (ROWS, STEPS, WIDE)
PAIRS = (SWEEPS - 2, 2, STEPS, WIDE)
EXTRA = [pltpu.VMEM((STEPS + 8, LANES), F32), pltpu.VMEM((4, ROWS, WIDE), F32)]


def call(kernel, name, flops, operands, shapes, scratch):
    return pl.pallas_call(
        kernel,
        name=name,
        out_shape=tuple(jax.ShapeDtypeStruct(shape, F32) for shape in shapes),
        in_specs=vmem(len(operands)),
        out_specs=tuple(vmem(len(shapes))),
        scratch_shapes=[pltpu.VMEM(shape, F32) for shape in scratch] + EXTRA,
        compiler_params=pltpu.CompilerParams(vmem_limit_bytes=24 * 1024 * 1024),
        cost_estimate=pl.CostEstimate(flops=flops, bytes_accessed=2**20, transcendentals=0),
    )(*operands)


def solve(up, own, down):
    fwd, inv, shifts = [jnp.asarray(table) for table in tables()]
    block = list(BLOCKS.values())
    main, *mine = call(own_kernel, "own", 10**7, (fwd, shifts, own), [(ROWS, STEPS, LANES)] + block + [FIELDS], [])
    low = call(below_kernel, "below", 2 * 10**7, (fwd, shifts, down) + tuple(mine), [(STEPS, WIDE), PAIRS], block + [FIELDS, (2, 2 * ROWS, STEPS, WIDE)])
    args = (fwd, inv, shifts, up, main) + tuple(mine) + tuple(low)
    return call(last_kernel, "last", 3 * 10**7, args, [(STEPS * ROWS, LANES)], block + [(ROWS + 1, STEPS, WIDE), (2, 2 * ROWS, STEPS, WIDE)])[0]


def place(received):
    return received.reshape(DEVS, LOCAL, ROWS, LANES).transpose(1, 2, 0, 3).reshape(LOCAL, ROWS, DEVS * LANES)


def local(iterate, initial, diffusion, courant_x, courant_y):
    t = lax.axis_index("tm").astype(jnp.int32).reshape(1)
    send = pack(t, iterate, initial, diffusion, courant_x, courant_y)
    count = lax.axis_size("space")
    down = [(i, i + 1) for i in range(count - 1)]
    up = [(i + 1, i) for i in range(count - 1)]
    own = lax.all_to_all(send, "tm", split_axis=0, concat_axis=0, tiled=True)
    own = own.reshape(DEVS * BLOCK, LANES)
    above = lax.ppermute(own, "space", down)
    below = lax.ppermute(own, "space", up)
    new = solve(above, own, below)
    back = lax.all_to_all(new.reshape(DEVS, LOCAL * ROWS, LANES), "tm", split_axis=0, concat_axis=0, tiled=True)
    return place(back)


def solution(mesh):
    return jax.shard_map(
        local,
        mesh=mesh,
        in_specs=(
            P("tm", "space", None),
            P("space", None),
            P("space", None),
            P("space", None),
            P("space", None),
        ),
        out_specs=P("tm", "space", None),
        check_vma=False,
    )
```

```python
import math

import jax
import jax.numpy as jnp
import numpy as np
from jax import lax
from jax.experimental import pallas as pl
from jax.experimental.pallas import tpu as pltpu
from jax.sharding import PartitionSpec as P

SWEEPS = 8
ALPHA = 0.01
STEPS = 64
HALF = STEPS // 2
DEVS = 16
LOCAL = STEPS // DEVS
ROWS = 8
LANES = 128
BLOCK = ROWS * LOCAL + ROWS
SPAN = 3 * ROWS
WIDE = 2 * LANES
F32 = jnp.float32


def tables():
    n = np.arange(STEPS)
    g = ALPHA ** (n / STEPS)
    k = np.arange(HALF)
    ang = 2.0 * np.pi * (np.outer(k, n) % STEPS) / STEPS
    fwd = np.concatenate([np.cos(ang) * g, -np.sin(ang) * g], 0)
    fwd[HALF] = (-1.0) ** n * g
    inv = np.concatenate([2.0 * np.cos(ang), -2.0 * np.sin(ang)], 0).T
    inv[:, 0] = 1.0
    inv[:, HALF] = (-1.0) ** n
    inv = inv / (STEPS * g[:, None])
    beta = ALPHA ** (1.0 / STEPS)
    shift_re = 1.0 - beta * np.cos(2.0 * np.pi * k / STEPS)
    shift_im = beta * np.sin(2.0 * np.pi * k / STEPS)
    shift_alt = shift_re.copy()
    shift_alt[0] = 1.0 + beta
    shifts = np.zeros((HALF, 3 * LANES), np.float32)
    shifts[:, :LANES] = shift_re[:, None]
    shifts[:, LANES : 2 * LANES] = shift_im[:, None]
    shifts[:, 2 * LANES :] = shift_alt[:, None]
    return fwd.astype(np.float32), inv.astype(np.float32), shifts


def lane_ids(rows):
    return lax.broadcasted_iota(jnp.int32, (rows, LANES), 1)


def rim(left, right):
    lane = lane_ids(ROWS)
    both = jnp.where(lane < 8, right, jnp.where(lane >= LANES - 8, left, 0.0))
    moved = pltpu.roll(both, 8, 1, stride=16, stride_axis=0)
    return jnp.sum(moved, axis=0, keepdims=True)


def pack_kernel(t_ref, it_ref, ini_ref, dif_ref, cx_ref, cy_ref, send_ref):
    t = t_ref[0]
    which, share = t % 4, t // 4
    coef = jnp.where(which < 2, jnp.where(which == 0, ini_ref[...], dif_ref[...]), jnp.where(which == 2, cx_ref[...], cy_ref[...]))
    turned = pltpu.roll(coef, (ROWS - 2 * share) % ROWS, 0)
    zero = jnp.zeros((ROWS, LANES), F32)

    def sides(cols, d):
        return rim(cols(d - 1) if d else zero, cols(d + 1) if d + 1 < DEVS else zero)

    for d in range(DEVS):
        rims = []
        for n in range(LOCAL):
            cols = lambda e: it_ref[n, :, e * LANES : (e + 1) * LANES]
            send_ref[d, n * ROWS : (n + 1) * ROWS, :] = cols(d)
            rims.append(sides(cols, d))
        rims.append(turned[:2, d * LANES : (d + 1) * LANES])
        rims.append(sides(lambda e: coef[:, e * LANES : (e + 1) * LANES], d))
        rims.append(jnp.zeros((1, LANES), F32))
        send_ref[d, LOCAL * ROWS :, :] = jnp.concatenate(rims, 0)


def mul(matrix, value):
    return jnp.dot(matrix, value, precision=lax.Precision.HIGHEST, preferred_element_type=F32)


def row(refs, j):
    return refs[j // ROWS].at[j % ROWS]


def build(ref, x_ref, wt_ref, rim_ref, coef_ref, main_ref=None):
    def tiles(main, turned):
        lane = lane_ids(main.shape[0])
        return jnp.where(lane >= LANES - 8, turned, main), jnp.where(lane < 8, turned, main)

    for d in range(DEVS):
        base = d * BLOCK + LOCAL * ROWS
        rim_ref[d * LOCAL : (d + 1) * LOCAL, :] = ref[base : base + LOCAL, :]
        share = 2 * (d // 4)
        coef_ref[d % 4, share : share + 2, :LANES] = ref[base + LOCAL : base + LOCAL + 2, :]
        if d < 4:
            rim_ref[STEPS + d : STEPS + d + 1, :] = ref[base + LOCAL + 2 : base + LOCAL + 3, :]
    rims = rim_ref[...]
    for r in range(ROWS):
        for d in range(DEVS):
            x_ref[r, 8 + d * LOCAL : 8 + (d + 1) * LOCAL, :LANES] = ref[pl.ds(d * BLOCK + r, LOCAL, stride=ROWS), :]
        turned = pltpu.roll(rims, (2 * LANES - 16 * r - 8) % LANES, 1)
        main = x_ref[r, 8:, :LANES]
        if main_ref is not None:
            main_ref[r] = main
        x_ref[r, 8:, :LANES], x_ref[r, 8:, LANES:] = tiles(main, turned[:STEPS])
        for a in range(4):
            one = slice(r, r + 1)
            coef_ref[a, one, :LANES], coef_ref[a, one, LANES:] = tiles(coef_ref[a, one, :LANES], turned[STEPS + a : STEPS + a + 1])
        x_ref[r, 7:8, :] = coef_ref[0, r : r + 1, :]
    dif, cx, cy = coef_ref[1], coef_ref[2], coef_ref[3]
    west = dif + jnp.maximum(cx, 0.0)
    east = dif + jnp.maximum(-cx, 0.0)
    north = dif + jnp.maximum(cy, 0.0)
    south = dif + jnp.maximum(-cy, 0.0)
    for a, value in enumerate((west, east, north, south, west + east + north + south)):
        wt_ref[a] = value


def diagonal(shift_ref, wt_ref, a_ref, alt_ref, b_ref, r):
    centre = wt_ref[4, r : r + 1, :]
    for g in range(HALF // 8):
        part = slice(8 * g, 8 * g + 8)
        rep = lambda c: jnp.concatenate([shift_ref[part, c * LANES : (c + 1) * LANES]] * 2, 1)
        s_im = rep(1)
        d_re = rep(0) + centre
        norm = 1.0 / (d_re * d_re + s_im * s_im)
        a_ref[r, part, :] = d_re * norm
        b_ref[r, part, :] = s_im * norm
        if g == 0:
            d_im = rep(2) + centre
            alt_ref[r] = d_im * (1.0 / (d_im * d_im + s_im * s_im))


def near(wts, here, above, below):
    west, east = [
        jnp.concatenate([pltpu.roll(here[:, :LANES], by, 1), pltpu.roll(here[:, LANES:], by, 1)], 1) for by in (1, LANES - 1)
    ]
    summed = wts[0] * west + wts[1] * east
    return summed + wts[2] * above + wts[3] * below


class Grid:
    def __init__(self, x, wt, a, alt, b):
        self.x, self.wt, self.a, self.alt, self.b = x, wt, a, alt, b

    def weights(self, j):
        ref, r = self.wt[j // ROWS], j % ROWS
        return [ref[a, r : r + 1, :] for a in range(5)]

    def divide(self, j, g, q_re, q_im):
        part = slice(8 * g, 8 * g + 8)
        a_re, b = row(self.a, j)[part, :], row(self.b, j)[part, :]
        a_im = row(self.alt, j)[...] if g == 0 else a_re
        return q_re * a_re + q_im * b, q_im * a_im - q_re * b

    def first(self, fwd_ref, j, dst):
        wts = self.weights(j)
        here = row(self.x, j)[8:, :]
        r = row(self.x, j)[7 : 7 + STEPS, :] - here
        r = r + near(wts, here, row(self.x, j - 1)[8:, :], row(self.x, j + 1)[8:, :]) - wts[4] * here
        hat = mul(fwd_ref[...], r)
        for g in range(HALF // 8):
            p_re, p_im = parts(g)
            dst[p_re, :], dst[p_im, :] = self.divide(j, g, hat[p_re], hat[p_im])

    def sweep(self, j, level, m):
        values = {}
        wts = self.weights(j)
        here, above, below = level(m - 1, j), level(m - 1, j - 1), level(m - 1, j + 1)
        base = level(1, j)
        for g in range(HALF // 8):
            sums = [near(wts, here[p, :], above[p, :], below[p, :]) for p in parts(g)]
            for p, value in zip(parts(g), self.divide(j, g, *sums)):
                values[p.start] = base[p, :] + value
        return values

    def store(self, j, level, m):
        dst = level(m, j)
        for start, value in self.sweep(j, level, m).items():
            dst[start : start + 8, :] = value


def parts(g):
    return slice(8 * g, 8 * g + 8), slice(HALF + 8 * g, HALF + 8 * g + 8)


def own_kernel(fwd_ref, shift_ref, own_ref, main_ref, x_ref, wt_ref, a_ref, alt_ref, b_ref, f_ref, rim_ref, coef_ref):
    build(own_ref, x_ref, wt_ref, rim_ref, coef_ref, main_ref)
    grid = Grid(*[(None, ref, None) for ref in (x_ref, wt_ref, a_ref, alt_ref, b_ref)])
    for r in range(ROWS):
        diagonal(shift_ref, wt_ref, a_ref, alt_ref, b_ref, r)
    for r in range(1, ROWS - 1):
        grid.first(fwd_ref, ROWS + r, f_ref.at[r])


def below_kernel(
    fwd_ref, shift_ref, dn_ref, x1, wt1, a1, alt1, b1, f1,
    f15_ref, edge_ref, x_ref, wt_ref, a_ref, alt_ref, b_ref, f_ref, w_ref, rim_ref, coef_ref,
):
    build(dn_ref, x_ref, wt_ref, rim_ref, coef_ref)
    grid = Grid((None, x1, x_ref), (None, wt1, wt_ref), (None, a1, a_ref), (None, alt1, alt_ref), (None, b1, b_ref))
    for r in range(ROWS - 1):
        diagonal(shift_ref, wt_ref, a_ref, alt_ref, b_ref, r)

    def level(m, j):
        if m == 1:
            return f1.at[j - 8] if j < 15 else f15_ref if j == 15 else f_ref.at[j - 16]
        return edge_ref.at[m - 2, j - 8 - m] if j <= 9 + m else w_ref.at[m % 2, j - 8]

    for j in range(15, SPAN - 1):
        grid.first(fwd_ref, j, level(1, j))
    for m in range(2, SWEEPS):
        for j in range(8 + m, SPAN - m):
            grid.store(j, level, m)


def last_kernel(
    fwd_ref, inv_ref, shift_ref, up_ref, main_ref, x1, wt1, a1, alt1, b1, f1, f15_ref, edge_ref,
    out_ref, x_ref, wt_ref, a_ref, alt_ref, b_ref, f_ref, w_ref, rim_ref, coef_ref,
):
    build(up_ref, x_ref, wt_ref, rim_ref, coef_ref)
    grid = Grid((x_ref, x1), (wt_ref, wt1), (a_ref, a1), (alt_ref, alt1), (b_ref, b1))
    for r in range(1, ROWS):
        diagonal(shift_ref, wt_ref, a_ref, alt_ref, b_ref, r)

    def level(m, j):
        if m == 1:
            return f_ref.at[j] if j <= 8 else f1.at[j - 8] if j < 15 else f15_ref
        return w_ref.at[m % 2, j] if j <= 7 + m else edge_ref.at[m - 2, j - 8 - m]

    for j in range(1, ROWS + 1):
        grid.first(fwd_ref, j, level(1, j))
    for m in range(2, SWEEPS):
        for j in range(m, 8 + m):
            grid.store(j, level, m)
    left = lane_ids(8) < LANES // 2

    def final(j):
        values = grid.sweep(j, level, SWEEPS)
        return jnp.concatenate([jnp.where(left, values[p][:, :LANES], values[p][:, LANES:]) for p in range(0, STEPS, 8)], 0)

    for r in range(0, ROWS, 2):
        corr = mul(inv_ref[...], jnp.concatenate([final(ROWS + r), final(ROWS + r + 1)], 1))
        for i in range(2):
            out_ref[pl.ds(r + i, STEPS, stride=ROWS), :] = main_ref[r + i] + corr[:, i * LANES : (i + 1) * LANES]


def vmem(count):
    return [pl.BlockSpec(memory_space=pltpu.VMEM)] * count


def pack(t, iterate, initial, diffusion, courant_x, courant_y):
    return pl.pallas_call(
        pack_kernel,
        name="pack",
        out_shape=pltpu.VMEM((DEVS, BLOCK, LANES), F32),
        in_specs=[pl.BlockSpec(memory_space=pltpu.SMEM)] + vmem(5),
        out_specs=vmem(1)[0],
    )(t, iterate, initial, diffusion, courant_x, courant_y)


BLOCKS = {
    "x": (ROWS, STEPS + 8, WIDE),
    "wt": (5, ROWS, WIDE),
    "a": (ROWS, HALF, WIDE),
    "alt": (ROWS, 8, WIDE),
    "b": (ROWS, HALF, WIDE),
}
FIELDS = (ROWS, STEPS, WIDE)
PAIRS = (SWEEPS - 2, 2, STEPS, WIDE)
EXTRA = [pltpu.VMEM((STEPS + 8, LANES), F32), pltpu.VMEM((4, ROWS, WIDE), F32)]


def call(kernel, name, flops, operands, shapes, scratch):
    return pl.pallas_call(
        kernel,
        name=name,
        out_shape=tuple(jax.ShapeDtypeStruct(shape, F32) for shape in shapes),
        in_specs=vmem(len(operands)),
        out_specs=tuple(vmem(len(shapes))),
        scratch_shapes=[pltpu.VMEM(shape, F32) for shape in scratch] + EXTRA,
        compiler_params=pltpu.CompilerParams(vmem_limit_bytes=24 * 1024 * 1024),
        cost_estimate=pl.CostEstimate(flops=flops, bytes_accessed=2**20, transcendentals=0),
    )(*operands)


def solve(up, own, down):
    fwd, inv, shifts = [jnp.asarray(table) for table in tables()]
    block = list(BLOCKS.values())
    main, *mine = call(own_kernel, "own", 10**7, (fwd, shifts, own), [(ROWS, STEPS, LANES)] + block + [FIELDS], [])
    low = call(below_kernel, "below", 2 * 10**7, (fwd, shifts, down) + tuple(mine), [(STEPS, WIDE), PAIRS], block + [FIELDS, (2, 2 * ROWS, STEPS, WIDE)])
    args = (fwd, inv, shifts, up, main) + tuple(mine) + tuple(low)
    return call(last_kernel, "last", 3 * 10**7, args, [(STEPS * ROWS, LANES)], block + [(ROWS + 1, STEPS, WIDE), (2, 2 * ROWS, STEPS, WIDE)])[0]


def place(received):
    return received.reshape(DEVS, LOCAL, ROWS, LANES).transpose(1, 2, 0, 3).reshape(LOCAL, ROWS, DEVS * LANES)


def local(iterate, initial, diffusion, courant_x, courant_y):
    t = lax.axis_index("tm").astype(jnp.int32).reshape(1)
    send = pack(t, iterate, initial, diffusion, courant_x, courant_y)
    count = lax.axis_size("space")
    down = [(i, i + 1) for i in range(count - 1)]
    up = [(i + 1, i) for i in range(count - 1)]
    own = lax.all_to_all(send, "tm", split_axis=0, concat_axis=0, tiled=True)
    own = own.reshape(DEVS * BLOCK, LANES)
    above = lax.ppermute(own, "space", down)
    below = lax.ppermute(own, "space", up)
    new = solve(above, own, below)
    back = lax.all_to_all(new.reshape(DEVS, LOCAL * ROWS, LANES), "tm", split_axis=0, concat_axis=0, tiled=True)
    return place(back)


def solution(mesh):
    return jax.shard_map(
        local,
        mesh=mesh,
        in_specs=(
            P("tm", "space", None),
            P("space", None),
            P("space", None),
            P("space", None),
            P("space", None),
        ),
        out_specs=P("tm", "space", None),
        check_vma=False,
    )
```

```python
import math

import jax
import jax.numpy as jnp
import numpy as np
from jax import lax
from jax.experimental import pallas as pl
from jax.experimental.pallas import tpu as pltpu
from jax.sharding import PartitionSpec as P

SWEEPS = 8
ALPHA = 0.01
STEPS = 64
HALF = STEPS // 2
DEVS = 16
LOCAL = STEPS // DEVS
ROWS = 8
LANES = 128
BLOCK = ROWS * LOCAL + ROWS
SPAN = 3 * ROWS
WIDE = 2 * LANES
F32 = jnp.float32


def tables():
    n = np.arange(STEPS)
    g = ALPHA ** (n / STEPS)
    k = np.arange(HALF)
    ang = 2.0 * np.pi * (np.outer(k, n) % STEPS) / STEPS
    fwd = np.concatenate([np.cos(ang) * g, -np.sin(ang) * g], 0)
    fwd[HALF] = (-1.0) ** n * g
    inv = np.concatenate([2.0 * np.cos(ang), -2.0 * np.sin(ang)], 0).T
    inv[:, 0] = 1.0
    inv[:, HALF] = (-1.0) ** n
    inv = inv / (STEPS * g[:, None])
    beta = ALPHA ** (1.0 / STEPS)
    shift_re = 1.0 - beta * np.cos(2.0 * np.pi * k / STEPS)
    shift_im = beta * np.sin(2.0 * np.pi * k / STEPS)
    shift_alt = shift_re.copy()
    shift_alt[0] = 1.0 + beta
    order = n.reshape(DEVS, LOCAL).T.reshape(-1)
    fwd, inv = fwd[:, order], inv[order]
    shifts = np.zeros((HALF, 3 * LANES), np.float32)
    shifts[:, :LANES] = shift_re[:, None]
    shifts[:, LANES : 2 * LANES] = shift_im[:, None]
    shifts[:, 2 * LANES :] = shift_alt[:, None]
    return fwd.astype(np.float32), inv.astype(np.float32), shifts


def lane_ids(rows):
    return lax.broadcasted_iota(jnp.int32, (rows, LANES), 1)


def rim(left, right):
    lane = lane_ids(ROWS)
    both = jnp.where(lane < 8, right, jnp.where(lane >= LANES - 8, left, 0.0))
    moved = pltpu.roll(both, 8, 1, stride=16, stride_axis=0)
    return jnp.sum(moved, axis=0, keepdims=True)


def flip(tile):
    row = lax.broadcasted_iota(jnp.int32, (ROWS, LANES), 0)
    return jnp.take_along_axis(tile, ROWS - 1 - row, axis=0)


def pack_kernel(t_ref, it_ref, ini_ref, dif_ref, cx_ref, cy_ref, send_ref):
    t = t_ref[0]
    which, share = t % 4, t // 4
    coef = jnp.where(which < 2, jnp.where(which == 0, ini_ref[...], dif_ref[...]), jnp.where(which == 2, cx_ref[...], cy_ref[...]))
    sign = jnp.where(which == 3, -1.0, 1.0)
    zero = jnp.zeros((ROWS, LANES), F32)

    def sides(tiles, d):
        return rim(tiles[d - 1] if d else zero, tiles[d + 1] if d + 1 < DEVS else zero)

    plain = [[it_ref[n, :, e * LANES : (e + 1) * LANES] for e in range(DEVS)] for n in range(LOCAL)]
    plain.append([coef[:, e * LANES : (e + 1) * LANES] for e in range(DEVS)])
    turned = [[flip(tile) for tile in tiles] for tiles in plain]
    turned[LOCAL] = [sign * tile for tile in turned[LOCAL]]
    for d in range(DEVS):
        tiles = turned if d % 2 else plain
        for n in range(LOCAL):
            send_ref[d, n * ROWS : (n + 1) * ROWS, :] = tiles[n][d]
        tail = [sides(tiles[n], d) for n in range(LOCAL)]
        tail.append(pltpu.roll(tiles[LOCAL][d], (ROWS - 2 * share) % ROWS, 0)[:2])
        tail.append(sides(tiles[LOCAL], d))
        send_ref[d, LOCAL * ROWS :, :] = jnp.concatenate(tail + [zero[:1]], 0)


def mul(matrix, value):
    return jnp.dot(matrix, value, precision=lax.Precision.HIGHEST, preferred_element_type=F32)


def row(refs, j):
    return refs[j // ROWS].at[j % ROWS]


def build(ref, x_ref, wt_ref, coef_ref, main_ref=None):
    def tiles(main, turned):
        lane = lane_ids(main.shape[0])
        return jnp.where(lane >= LANES - 8, turned, main), jnp.where(lane < 8, turned, main)

    def steps(offset, stride):
        starts = [half * 8 * BLOCK + n * stride + offset for n in range(LOCAL) for half in range(2)]
        return jnp.concatenate([ref[pl.ds(start, 8, stride=BLOCK), :] for start in starts], 0)

    for d in range(DEVS):
        base, share = d * BLOCK + (ROWS + 1) * LOCAL, 2 * (d // 4)
        coef_ref[d % 4, share : share + 2, :LANES] = ref[base : base + 2, :]
    rims = jnp.concatenate([steps(ROWS * LOCAL, 1), ref[pl.ds((ROWS + 1) * LOCAL + 2, 4, stride=BLOCK), :]], 0)
    for r in range(ROWS):
        main = steps(r, ROWS)
        if main_ref is not None:
            main_ref[r] = main
        turned = pltpu.roll(rims, (2 * LANES - 16 * r - 8) % LANES, 1)
        x_ref[r, DEVS:, :LANES], x_ref[r, DEVS:, LANES:] = tiles(main, turned[:STEPS])
        for a in range(4):
            one = slice(r, r + 1)
            coef_ref[a, one, :LANES], coef_ref[a, one, LANES:] = tiles(coef_ref[a, one, :LANES], turned[STEPS + a : STEPS + a + 1])
        x_ref[r, :1, :] = coef_ref[0, r : r + 1, :]
        x_ref[r, 1:DEVS, :] = x_ref[r, STEPS : STEPS + DEVS - 1, :]
    dif, cx, cy = coef_ref[1], coef_ref[2], coef_ref[3]
    west = dif + jnp.maximum(cx, 0.0)
    east = dif + jnp.maximum(-cx, 0.0)
    north = dif + jnp.maximum(cy, 0.0)
    south = dif + jnp.maximum(-cy, 0.0)
    for a, value in enumerate((west, east, north, south, west + east + north + south)):
        wt_ref[a] = value


def diagonal(shift_ref, wt_ref, a_ref, alt_ref, b_ref, r):
    centre = wt_ref[4, r : r + 1, :]
    for g in range(HALF // 8):
        part = slice(8 * g, 8 * g + 8)
        rep = lambda c: jnp.concatenate([shift_ref[part, c * LANES : (c + 1) * LANES]] * 2, 1)
        s_im = rep(1)
        d_re = rep(0) + centre
        norm = 1.0 / (d_re * d_re + s_im * s_im)
        a_ref[r, part, :] = d_re * norm
        b_ref[r, part, :] = s_im * norm
        if g == 0:
            d_im = rep(2) + centre
            alt_ref[r] = d_im * (1.0 / (d_im * d_im + s_im * s_im))


def near(wts, here, above, below):
    west, east = [
        jnp.concatenate([pltpu.roll(here[:, :LANES], by, 1), pltpu.roll(here[:, LANES:], by, 1)], 1) for by in (1, LANES - 1)
    ]
    summed = wts[0] * west + wts[1] * east
    return summed + wts[2] * above + wts[3] * below


class Grid:
    def __init__(self, x, wt, a, alt, b):
        self.x, self.wt, self.a, self.alt, self.b = x, wt, a, alt, b

    def weights(self, j):
        ref, r = self.wt[j // ROWS], j % ROWS
        return [ref[a, r : r + 1, :] for a in range(5)]

    def divide(self, j, g, q_re, q_im):
        part = slice(8 * g, 8 * g + 8)
        a_re, b = row(self.a, j)[part, :], row(self.b, j)[part, :]
        a_im = row(self.alt, j)[...] if g == 0 else a_re
        return q_re * a_re + q_im * b, q_im * a_im - q_re * b

    def first(self, fwd_ref, j, dst):
        wts = self.weights(j)
        here = row(self.x, j)[DEVS:, :]
        r = row(self.x, j)[:STEPS, :] - here
        r = r + near(wts, here, row(self.x, j - 1)[DEVS:, :], row(self.x, j + 1)[DEVS:, :]) - wts[4] * here
        hat = mul(fwd_ref[...], r)
        for g in range(HALF // 8):
            p_re, p_im = parts(g)
            dst[p_re, :], dst[p_im, :] = self.divide(j, g, hat[p_re], hat[p_im])

    def sweep(self, j, level, m):
        values = {}
        wts = self.weights(j)
        here, above, below = level(m - 1, j), level(m - 1, j - 1), level(m - 1, j + 1)
        base = level(1, j)
        for g in range(HALF // 8):
            sums = [near(wts, here[p, :], above[p, :], below[p, :]) for p in parts(g)]
            for p, value in zip(parts(g), self.divide(j, g, *sums)):
                values[p.start] = base[p, :] + value
        return values

    def store(self, j, level, m):
        dst = level(m, j)
        for start, value in self.sweep(j, level, m).items():
            dst[start : start + 8, :] = value


def parts(g):
    return slice(8 * g, 8 * g + 8), slice(HALF + 8 * g, HALF + 8 * g + 8)


def own_kernel(fwd_ref, shift_ref, own_ref, main_ref, x_ref, wt_ref, a_ref, alt_ref, b_ref, f_ref, coef_ref):
    build(own_ref, x_ref, wt_ref, coef_ref, main_ref)
    grid = Grid(*[(None, ref, None) for ref in (x_ref, wt_ref, a_ref, alt_ref, b_ref)])
    for r in range(ROWS):
        diagonal(shift_ref, wt_ref, a_ref, alt_ref, b_ref, r)
    for r in range(1, ROWS - 1):
        grid.first(fwd_ref, ROWS + r, f_ref.at[r])


def below_kernel(
    fwd_ref, shift_ref, dn_ref, x1, wt1, a1, alt1, b1, f1,
    f15_ref, edge_ref, x_ref, wt_ref, a_ref, alt_ref, b_ref, f_ref, w_ref, coef_ref,
):
    build(dn_ref, x_ref, wt_ref, coef_ref)
    grid = Grid((None, x1, x_ref), (None, wt1, wt_ref), (None, a1, a_ref), (None, alt1, alt_ref), (None, b1, b_ref))
    for r in range(ROWS - 1):
        diagonal(shift_ref, wt_ref, a_ref, alt_ref, b_ref, r)

    def level(m, j):
        if m == 1:
            return f1.at[j - 8] if j < 15 else f15_ref if j == 15 else f_ref.at[j - 16]
        return edge_ref.at[m - 2, j - 8 - m] if j <= 9 + m else w_ref.at[m % 2, j - 8]

    for j in range(15, SPAN - 1):
        grid.first(fwd_ref, j, level(1, j))
    for m in range(2, SWEEPS):
        for j in range(8 + m, SPAN - m):
            grid.store(j, level, m)


def last_kernel(
    t_ref, fwd_ref, inv_ref, shift_ref, up_ref, main_ref, x1, wt1, a1, alt1, b1, f1, f15_ref, edge_ref,
    out_ref, x_ref, wt_ref, a_ref, alt_ref, b_ref, f_ref, w_ref, coef_ref,
):
    build(up_ref, x_ref, wt_ref, coef_ref)
    grid = Grid((x_ref, x1), (wt_ref, wt1), (a_ref, a1), (alt_ref, alt1), (b_ref, b1))
    for r in range(1, ROWS):
        diagonal(shift_ref, wt_ref, a_ref, alt_ref, b_ref, r)

    def level(m, j):
        if m == 1:
            return f_ref.at[j] if j <= 8 else f1.at[j - 8] if j < 15 else f15_ref
        return w_ref.at[m % 2, j] if j <= 7 + m else edge_ref.at[m - 2, j - 8 - m]

    for j in range(1, ROWS + 1):
        grid.first(fwd_ref, j, level(1, j))
    for m in range(2, SWEEPS):
        for j in range(m, 8 + m):
            grid.store(j, level, m)
    left = lane_ids(8) < LANES // 2

    def final(j):
        values = grid.sweep(j, level, SWEEPS)
        return jnp.concatenate([jnp.where(left, values[p][:, :LANES], values[p][:, LANES:]) for p in range(0, STEPS, 8)], 0)

    for r in range(0, ROWS, 2):
        corr = mul(inv_ref[...], jnp.concatenate([final(ROWS + r), final(ROWS + r + 1)], 1))
        for i in range(2):
            new = main_ref[r + i] + corr[:, i * LANES : (i + 1) * LANES]
            place = jnp.where(t_ref[0] % 2 == 0, r + i, ROWS - 1 - r - i)
            for n in range(LOCAL):
                out_ref[pl.ds(n * ROWS + place, DEVS, stride=ROWS * LOCAL), :] = new[n * DEVS : (n + 1) * DEVS]


def vmem(count):
    return [pl.BlockSpec(memory_space=pltpu.VMEM)] * count


def pack(t, iterate, initial, diffusion, courant_x, courant_y):
    return pl.pallas_call(
        pack_kernel,
        name="pack",
        out_shape=pltpu.VMEM((DEVS, BLOCK, LANES), F32),
        in_specs=[pl.BlockSpec(memory_space=pltpu.SMEM)] + vmem(5),
        out_specs=vmem(1)[0],
    )(t, iterate, initial, diffusion, courant_x, courant_y)


BLOCKS = {
    "x": (ROWS, STEPS + DEVS, WIDE),
    "wt": (5, ROWS, WIDE),
    "a": (ROWS, HALF, WIDE),
    "alt": (ROWS, 8, WIDE),
    "b": (ROWS, HALF, WIDE),
}
FIELDS = (ROWS, STEPS, WIDE)
PAIRS = (SWEEPS - 2, 2, STEPS, WIDE)
EXTRA = [pltpu.VMEM((4, ROWS, WIDE), F32)]


def call(kernel, name, flops, operands, shapes, scratch, scalars=0):
    return pl.pallas_call(
        kernel,
        name=name,
        out_shape=tuple(jax.ShapeDtypeStruct(shape, F32) for shape in shapes),
        in_specs=[pl.BlockSpec(memory_space=pltpu.SMEM)] * scalars + vmem(len(operands) - scalars),
        out_specs=tuple(vmem(len(shapes))),
        scratch_shapes=[pltpu.VMEM(shape, F32) for shape in scratch] + EXTRA,
        compiler_params=pltpu.CompilerParams(vmem_limit_bytes=24 * 1024 * 1024),
        cost_estimate=pl.CostEstimate(flops=flops, bytes_accessed=2**20, transcendentals=0),
    )(*operands)


def solve(t, above, own, below):
    fwd, inv, shifts = [jnp.asarray(table) for table in tables()]
    block = list(BLOCKS.values())
    main, *mine = call(own_kernel, "own", 10**7, (fwd, shifts, own), [(ROWS, STEPS, LANES)] + block + [FIELDS], [])
    low = call(below_kernel, "below", 2 * 10**7, (fwd, shifts, below) + tuple(mine), [(STEPS, WIDE), PAIRS], block + [FIELDS, (2, 2 * ROWS, STEPS, WIDE)])
    args = (t, fwd, inv, shifts, above, main) + tuple(mine) + tuple(low)
    return call(last_kernel, "last", 3 * 10**7, args, [(STEPS * ROWS, LANES)], block + [(ROWS + 1, STEPS, WIDE), (2, 2 * ROWS, STEPS, WIDE)], 1)[0]


def place(received):
    return received.reshape(DEVS, LOCAL, ROWS, LANES).transpose(1, 2, 0, 3).reshape(LOCAL, ROWS, DEVS * LANES)


def local(iterate, initial, diffusion, courant_x, courant_y):
    t = lax.axis_index("tm").astype(jnp.int32).reshape(1)
    send = pack(t, iterate, initial, diffusion, courant_x, courant_y)
    own = lax.all_to_all(send, "tm", split_axis=0, concat_axis=0, tiled=True)
    own = own.reshape(DEVS * BLOCK, LANES)
    count, halo = lax.axis_size("space"), []
    for way in (1, 0):
        pairs = []
        for d in range(DEVS):
            for i in range(count - 1):
                lower, upper = d * count + i + 1, d * count + i
                pairs.append((upper, lower) if d % 2 == way else (lower, upper))
        halo.append(lax.ppermute(own, ("tm", "space"), pairs))
    below, above = halo
    new = solve(t, above, own, below)
    back = lax.all_to_all(new.reshape(DEVS, LOCAL * ROWS, LANES), "tm", split_axis=0, concat_axis=0, tiled=True)
    return place(back)


def solution(mesh):
    return jax.shard_map(
        local,
        mesh=mesh,
        in_specs=(
            P("tm", "space", None),
            P("space", None),
            P("space", None),
            P("space", None),
            P("space", None),
        ),
        out_specs=P("tm", "space", None),
        check_vma=False,
    )
```

```python
import math

import jax
import jax.numpy as jnp
import numpy as np
from jax import lax
from jax.experimental import pallas as pl
from jax.experimental.pallas import tpu as pltpu
from jax.sharding import PartitionSpec as P

SWEEPS = 8
ALPHA = 0.01
STEPS = 64
HALF = STEPS // 2
DEVS = 16
LOCAL = STEPS // DEVS
ROWS = 8
LANES = 128
BLOCK = ROWS * LOCAL + ROWS
SPAN = 3 * ROWS
WIDE = 2 * LANES
F32 = jnp.float32
BF16 = jnp.bfloat16


def tables():
    n = np.arange(STEPS)
    g = ALPHA ** (n / STEPS)
    k = np.arange(HALF)
    ang = 2.0 * np.pi * (np.outer(k, n) % STEPS) / STEPS
    fwd = np.concatenate([np.cos(ang) * g, -np.sin(ang) * g], 0)
    fwd[HALF] = (-1.0) ** n * g
    inv = np.concatenate([2.0 * np.cos(ang), -2.0 * np.sin(ang)], 0).T
    inv[:, 0] = 1.0
    inv[:, HALF] = (-1.0) ** n
    inv = inv / (STEPS * g[:, None])
    beta = ALPHA ** (1.0 / STEPS)
    shift_re = 1.0 - beta * np.cos(2.0 * np.pi * k / STEPS)
    shift_im = beta * np.sin(2.0 * np.pi * k / STEPS)
    shift_alt = shift_re.copy()
    shift_alt[0] = 1.0 + beta
    order = n.reshape(DEVS, LOCAL).T.reshape(-1)
    fwd, inv = fwd[:, order], inv[order]
    shifts = np.zeros((HALF, 3 * LANES), np.float32)
    shifts[:, :LANES] = shift_re[:, None]
    shifts[:, LANES : 2 * LANES] = shift_im[:, None]
    shifts[:, 2 * LANES :] = shift_alt[:, None]
    return fwd.astype(np.float32), inv.astype(np.float32), shifts


def lane_ids(rows):
    return lax.broadcasted_iota(jnp.int32, (rows, LANES), 1)


def rim(left, right):
    lane = lane_ids(ROWS)
    both = jnp.where(lane < 8, right, jnp.where(lane >= LANES - 8, left, 0.0))
    moved = pltpu.roll(both, 8, 1, stride=16, stride_axis=0)
    return jnp.sum(moved, axis=0, keepdims=True)


def flip(tile):
    row = lax.broadcasted_iota(jnp.int32, (ROWS, LANES), 0)
    return jnp.take_along_axis(tile, ROWS - 1 - row, axis=0)


def pack_kernel(t_ref, it_ref, ini_ref, dif_ref, cx_ref, cy_ref, send_ref):
    t = t_ref[0]
    which, share = t % 4, t // 4
    coef = jnp.where(which < 2, jnp.where(which == 0, ini_ref[...], dif_ref[...]), jnp.where(which == 2, cx_ref[...], cy_ref[...]))
    sign = jnp.where(which == 3, -1.0, 1.0)
    zero = jnp.zeros((ROWS, LANES), F32)

    def sides(tiles, d):
        return rim(tiles[d - 1] if d else zero, tiles[d + 1] if d + 1 < DEVS else zero)

    plain = [[it_ref[n, :, e * LANES : (e + 1) * LANES] for e in range(DEVS)] for n in range(LOCAL)]
    plain.append([coef[:, e * LANES : (e + 1) * LANES] for e in range(DEVS)])
    turned = [[flip(tile) for tile in tiles] for tiles in plain]
    turned[LOCAL] = [sign * tile for tile in turned[LOCAL]]
    for d in range(DEVS):
        tiles = turned if d % 2 else plain
        for n in range(LOCAL):
            send_ref[d, n * ROWS : (n + 1) * ROWS, :] = tiles[n][d]
        tail = [sides(tiles[n], d) for n in range(LOCAL)]
        tail.append(pltpu.roll(tiles[LOCAL][d], (ROWS - 2 * share) % ROWS, 0)[:2])
        tail.append(sides(tiles[LOCAL], d))
        send_ref[d, LOCAL * ROWS :, :] = jnp.concatenate(tail + [zero[:1]], 0)


def pieces(value):
    first = value.astype(BF16)
    rest = value - first.astype(F32)
    second = rest.astype(BF16)
    return first, second, (rest - second.astype(F32)).astype(BF16)


def stacked(table):
    one, two, three = [np.asarray(part) for part in pieces(table)]
    return np.concatenate([one, two, one, two, one, three], 1)


def mul(matrix, value):
    one, two, three = pieces(value)
    parts_of = jnp.concatenate([one, one, two, two, three, one], 0)
    return jnp.dot(matrix, parts_of, preferred_element_type=F32)


def row(refs, j):
    return refs[j // ROWS].at[j % ROWS]


def build(ref, x_ref, wt_ref, coef_ref, main_ref=None):
    def tiles(main, turned):
        lane = lane_ids(main.shape[0])
        return jnp.where(lane >= LANES - 8, turned, main), jnp.where(lane < 8, turned, main)

    def steps(offset, stride):
        starts = [half * 8 * BLOCK + n * stride + offset for n in range(LOCAL) for half in range(2)]
        return jnp.concatenate([ref[pl.ds(start, 8, stride=BLOCK), :] for start in starts], 0)

    for d in range(DEVS):
        base, share = d * BLOCK + (ROWS + 1) * LOCAL, 2 * (d // 4)
        coef_ref[d % 4, share : share + 2, :LANES] = ref[base : base + 2, :]
    rims = jnp.concatenate([steps(ROWS * LOCAL, 1), ref[pl.ds((ROWS + 1) * LOCAL + 2, 4, stride=BLOCK), :]], 0)
    for r in range(ROWS):
        main = steps(r, ROWS)
        if main_ref is not None:
            main_ref[r] = main
        turned = pltpu.roll(rims, (2 * LANES - 16 * r - 8) % LANES, 1)
        x_ref[r, DEVS:, :LANES], x_ref[r, DEVS:, LANES:] = tiles(main, turned[:STEPS])
        for a in range(4):
            one = slice(r, r + 1)
            coef_ref[a, one, :LANES], coef_ref[a, one, LANES:] = tiles(coef_ref[a, one, :LANES], turned[STEPS + a : STEPS + a + 1])
        x_ref[r, :1, :] = coef_ref[0, r : r + 1, :]
        x_ref[r, 1:DEVS, :] = x_ref[r, STEPS : STEPS + DEVS - 1, :]
    dif, cx, cy = coef_ref[1], coef_ref[2], coef_ref[3]
    west = dif + jnp.maximum(cx, 0.0)
    east = dif + jnp.maximum(-cx, 0.0)
    north = dif + jnp.maximum(cy, 0.0)
    south = dif + jnp.maximum(-cy, 0.0)
    for a, value in enumerate((west, east, north, south, west + east + north + south)):
        wt_ref[a] = value


def diagonal(shift_ref, wt_ref, a_ref, alt_ref, b_ref, r):
    centre = wt_ref[4, r : r + 1, :]
    for g in range(HALF // 8):
        part = slice(8 * g, 8 * g + 8)
        rep = lambda c: jnp.concatenate([shift_ref[part, c * LANES : (c + 1) * LANES]] * 2, 1)
        s_im = rep(1)
        d_re = rep(0) + centre
        norm = 1.0 / (d_re * d_re + s_im * s_im)
        a_ref[r, part, :] = d_re * norm
        b_ref[r, part, :] = s_im * norm
        if g == 0:
            d_im = rep(2) + centre
            alt_ref[r] = d_im * (1.0 / (d_im * d_im + s_im * s_im))


def near(wts, here, above, below):
    west, east = [
        jnp.concatenate([pltpu.roll(here[:, :LANES], by, 1), pltpu.roll(here[:, LANES:], by, 1)], 1) for by in (1, LANES - 1)
    ]
    summed = wts[0] * west + wts[1] * east
    return summed + wts[2] * above + wts[3] * below


class Grid:
    def __init__(self, x, wt, a, alt, b):
        self.x, self.wt, self.a, self.alt, self.b = x, wt, a, alt, b

    def weights(self, j):
        ref, r = self.wt[j // ROWS], j % ROWS
        return [ref[a, r : r + 1, :] for a in range(5)]

    def divide(self, j, g, q_re, q_im):
        part = slice(8 * g, 8 * g + 8)
        a_re, b = row(self.a, j)[part, :], row(self.b, j)[part, :]
        a_im = row(self.alt, j)[...] if g == 0 else a_re
        return q_re * a_re + q_im * b, q_im * a_im - q_re * b

    def first(self, fwd_ref, j, dst):
        wts = self.weights(j)
        here = row(self.x, j)[DEVS:, :]
        r = row(self.x, j)[:STEPS, :] - here
        r = r + near(wts, here, row(self.x, j - 1)[DEVS:, :], row(self.x, j + 1)[DEVS:, :]) - wts[4] * here
        hat = mul(fwd_ref[...], r)
        for g in range(HALF // 8):
            p_re, p_im = parts(g)
            dst[p_re, :], dst[p_im, :] = self.divide(j, g, hat[p_re], hat[p_im])

    def sweep(self, j, level, m):
        values = {}
        wts = self.weights(j)
        here, above, below = level(m - 1, j), level(m - 1, j - 1), level(m - 1, j + 1)
        base = level(1, j)
        for g in range(HALF // 8):
            sums = [near(wts, here[p, :], above[p, :], below[p, :]) for p in parts(g)]
            for p, value in zip(parts(g), self.divide(j, g, *sums)):
                values[p.start] = base[p, :] + value
        return values

    def store(self, j, level, m):
        dst = level(m, j)
        for start, value in self.sweep(j, level, m).items():
            dst[start : start + 8, :] = value


def parts(g):
    return slice(8 * g, 8 * g + 8), slice(HALF + 8 * g, HALF + 8 * g + 8)


def early(m, j):
    return (m - 2) * 4 + j - 8 - m if m in (2, 3) and 8 + m <= j < 16 - m else None


def own_kernel(
    fwd_ref, shift_ref, own_ref, main_ref, x_ref, wt_ref, a_ref, alt_ref, b_ref, f_ref, early_ref, coef_ref
):
    build(own_ref, x_ref, wt_ref, coef_ref, main_ref)
    grid = Grid(*[(None, ref, None) for ref in (x_ref, wt_ref, a_ref, alt_ref, b_ref)])
    for r in range(ROWS):
        diagonal(shift_ref, wt_ref, a_ref, alt_ref, b_ref, r)
    for r in range(1, ROWS - 1):
        grid.first(fwd_ref, ROWS + r, f_ref.at[r])

    def level(m, j):
        return f_ref.at[j - 8] if m == 1 else early_ref.at[early(m, j)]

    for m in (2, 3):
        for j in range(8 + m, 16 - m):
            grid.store(j, level, m)


def below_kernel(
    fwd_ref, shift_ref, dn_ref, x1, wt1, a1, alt1, b1, f1, early_ref,
    f15_ref, edge_ref, x_ref, wt_ref, a_ref, alt_ref, b_ref, f_ref, w_ref, coef_ref,
):
    build(dn_ref, x_ref, wt_ref, coef_ref)
    grid = Grid((None, x1, x_ref), (None, wt1, wt_ref), (None, a1, a_ref), (None, alt1, alt_ref), (None, b1, b_ref))
    for r in range(ROWS - 1):
        diagonal(shift_ref, wt_ref, a_ref, alt_ref, b_ref, r)

    def level(m, j):
        if m == 1:
            return f1.at[j - 8] if j < 15 else f15_ref if j == 15 else f_ref.at[j - 16]
        if early(m, j) is not None:
            return early_ref.at[early(m, j)]
        return edge_ref.at[m - 4, j - 8 - m] if j <= 9 + m else w_ref.at[m % 2, j - 8]

    for j in range(15, SPAN - 1):
        grid.first(fwd_ref, j, level(1, j))
    for m in range(2, SWEEPS):
        for j in range(8 + m, SPAN - m):
            if early(m, j) is None:
                grid.store(j, level, m)


def last_kernel(
    t_ref, fwd_ref, inv_ref, shift_ref, up_ref, main_ref, x1, wt1, a1, alt1, b1, f1, early_ref, f15_ref, edge_ref,
    out_ref, x_ref, wt_ref, a_ref, alt_ref, b_ref, f_ref, w_ref, coef_ref,
):
    build(up_ref, x_ref, wt_ref, coef_ref)
    grid = Grid((x_ref, x1), (wt_ref, wt1), (a_ref, a1), (alt_ref, alt1), (b_ref, b1))
    for r in range(1, ROWS):
        diagonal(shift_ref, wt_ref, a_ref, alt_ref, b_ref, r)

    def level(m, j):
        if m == 1:
            return f_ref.at[j] if j <= 8 else f1.at[j - 8] if j < 15 else f15_ref
        if early(m, j) is not None:
            return early_ref.at[early(m, j)]
        return w_ref.at[m % 2, j] if j <= 7 + m else edge_ref.at[m - 4, j - 8 - m]

    for j in range(1, ROWS + 1):
        grid.first(fwd_ref, j, level(1, j))
    for m in range(2, SWEEPS):
        for j in range(m, 8 + m):
            grid.store(j, level, m)
    left = lane_ids(8) < LANES // 2

    def final(j):
        values = grid.sweep(j, level, SWEEPS)
        return jnp.concatenate([jnp.where(left, values[p][:, :LANES], values[p][:, LANES:]) for p in range(0, STEPS, 8)], 0)

    for r in range(0, ROWS, 2):
        corr = mul(inv_ref[...], jnp.concatenate([final(ROWS + r), final(ROWS + r + 1)], 1))
        for i in range(2):
            new = main_ref[r + i] + corr[:, i * LANES : (i + 1) * LANES]
            place = jnp.where(t_ref[0] % 2 == 0, r + i, ROWS - 1 - r - i)
            for n in range(LOCAL):
                out_ref[pl.ds(n * ROWS + place, DEVS, stride=ROWS * LOCAL), :] = new[n * DEVS : (n + 1) * DEVS]


def vmem(count):
    return [pl.BlockSpec(memory_space=pltpu.VMEM)] * count


def pack(t, iterate, initial, diffusion, courant_x, courant_y):
    return pl.pallas_call(
        pack_kernel,
        name="pack",
        out_shape=pltpu.VMEM((DEVS, BLOCK, LANES), F32),
        in_specs=[pl.BlockSpec(memory_space=pltpu.SMEM)] + vmem(5),
        out_specs=vmem(1)[0],
    )(t, iterate, initial, diffusion, courant_x, courant_y)


BLOCKS = {
    "x": (ROWS, STEPS + DEVS, WIDE),
    "wt": (5, ROWS, WIDE),
    "a": (ROWS, HALF, WIDE),
    "alt": (ROWS, 8, WIDE),
    "b": (ROWS, HALF, WIDE),
}
FIELDS = (ROWS, STEPS, WIDE)
PAIRS = (SWEEPS - 4, 2, STEPS, WIDE)
EXTRA = [pltpu.VMEM((4, ROWS, WIDE), F32)]


def call(kernel, name, flops, operands, shapes, scratch, scalars=0):
    return pl.pallas_call(
        kernel,
        name=name,
        out_shape=tuple(jax.ShapeDtypeStruct(shape, F32) for shape in shapes),
        in_specs=[pl.BlockSpec(memory_space=pltpu.SMEM)] * scalars + vmem(len(operands) - scalars),
        out_specs=tuple(vmem(len(shapes))),
        scratch_shapes=[pltpu.VMEM(shape, F32) for shape in scratch] + EXTRA,
        compiler_params=pltpu.CompilerParams(vmem_limit_bytes=24 * 1024 * 1024),
        cost_estimate=pl.CostEstimate(flops=flops, bytes_accessed=2**20, transcendentals=0),
    )(*operands)


def solve(t, above, own, below):
    fwd, inv, shifts = tables()
    fwd, inv, shifts = jnp.asarray(stacked(fwd)), jnp.asarray(stacked(inv)), jnp.asarray(shifts)
    block = list(BLOCKS.values())
    main, *mine = call(own_kernel, "own", 10**7, (fwd, shifts, own), [(ROWS, STEPS, LANES)] + block + [FIELDS, (6, STEPS, WIDE)], [])
    low = call(below_kernel, "below", 2 * 10**7, (fwd, shifts, below) + tuple(mine), [(STEPS, WIDE), PAIRS], block + [FIELDS, (2, 2 * ROWS, STEPS, WIDE)])
    args = (t, fwd, inv, shifts, above, main) + tuple(mine) + tuple(low)
    return call(last_kernel, "last", 3 * 10**7, args, [(STEPS * ROWS, LANES)], block + [(ROWS + 1, STEPS, WIDE), (2, 2 * ROWS, STEPS, WIDE)], 1)[0]


def place(received):
    return received.reshape(DEVS, LOCAL, ROWS, LANES).transpose(1, 2, 0, 3).reshape(LOCAL, ROWS, DEVS * LANES)


def local(iterate, initial, diffusion, courant_x, courant_y):
    t = lax.axis_index("tm").astype(jnp.int32).reshape(1)
    send = pack(t, iterate, initial, diffusion, courant_x, courant_y)
    own = lax.all_to_all(send, "tm", split_axis=0, concat_axis=0, tiled=True)
    own = own.reshape(DEVS * BLOCK, LANES)
    count, halo = lax.axis_size("space"), []
    for way in (1, 0):
        pairs = []
        for d in range(DEVS):
            for i in range(count - 1):
                lower, upper = d * count + i + 1, d * count + i
                pairs.append((upper, lower) if d % 2 == way else (lower, upper))
        halo.append(lax.ppermute(own, ("tm", "space"), pairs))
    below, above = halo
    new = solve(t, above, own, below)
    back = lax.all_to_all(new.reshape(DEVS, LOCAL * ROWS, LANES), "tm", split_axis=0, concat_axis=0, tiled=True)
    return place(back)


def solution(mesh):
    return jax.shard_map(
        local,
        mesh=mesh,
        in_specs=(
            P("tm", "space", None),
            P("space", None),
            P("space", None),
            P("space", None),
            P("space", None),
        ),
        out_specs=P("tm", "space", None),
        check_vma=False,
    )
```

```python
import math

import jax
import jax.numpy as jnp
import numpy as np
from jax import lax
from jax.experimental import pallas as pl
from jax.experimental.pallas import tpu as pltpu
from jax.sharding import PartitionSpec as P

SWEEPS = 8
ALPHA = 0.01
STEPS = 64
HALF = STEPS // 2
DEVS = 16
LOCAL = STEPS // DEVS
ROWS = 8
LANES = 128
BLOCK = ROWS * LOCAL + ROWS
SPAN = 3 * ROWS
WIDE = 2 * LANES
TILES = (slice(0, LANES), slice(LANES, WIDE))
F32 = jnp.float32
BF16 = jnp.bfloat16


def tables():
    n = np.arange(STEPS)
    g = ALPHA ** (n / STEPS)
    k = np.arange(HALF)
    ang = 2.0 * np.pi * (np.outer(k, n) % STEPS) / STEPS
    fwd = np.concatenate([np.cos(ang) * g, -np.sin(ang) * g], 0)
    fwd[HALF] = (-1.0) ** n * g
    inv = np.concatenate([2.0 * np.cos(ang), -2.0 * np.sin(ang)], 0).T
    inv[:, 0] = 1.0
    inv[:, HALF] = (-1.0) ** n
    inv = inv / (STEPS * g[:, None])
    beta = ALPHA ** (1.0 / STEPS)
    shift_re = 1.0 - beta * np.cos(2.0 * np.pi * k / STEPS)
    shift_im = beta * np.sin(2.0 * np.pi * k / STEPS)
    shift_alt = shift_re.copy()
    shift_alt[0] = 1.0 + beta
    order = n.reshape(DEVS, LOCAL).T.reshape(-1)
    fwd, inv = fwd[:, order], inv[order]
    shifts = np.zeros((HALF, 3 * LANES), np.float32)
    shifts[:, :LANES] = shift_re[:, None]
    shifts[:, LANES : 2 * LANES] = shift_im[:, None]
    shifts[:, 2 * LANES :] = shift_alt[:, None]
    return fwd.astype(np.float32), inv.astype(np.float32), shifts


def lane_ids(rows):
    return lax.broadcasted_iota(jnp.int32, (rows, LANES), 1)


def rim(left, right):
    lane = lane_ids(ROWS)
    both = jnp.where(lane < 8, right, jnp.where(lane >= LANES - 8, left, 0.0))
    moved = pltpu.roll(both, 8, 1, stride=16, stride_axis=0)
    return jnp.sum(moved, axis=0, keepdims=True)


def flip(tile):
    row = lax.broadcasted_iota(jnp.int32, (ROWS, LANES), 0)
    return jnp.take_along_axis(tile, ROWS - 1 - row, axis=0)


def pack_kernel(t_ref, it_ref, ini_ref, dif_ref, cx_ref, cy_ref, send_ref):
    t = t_ref[0]
    which, share = t % 4, t // 4
    coef = jnp.where(which < 2, jnp.where(which == 0, ini_ref[...], dif_ref[...]), jnp.where(which == 2, cx_ref[...], cy_ref[...]))
    sign = jnp.where(which == 3, -1.0, 1.0)
    zero = jnp.zeros((ROWS, LANES), F32)

    def sides(tiles, d):
        return rim(tiles[d - 1] if d else zero, tiles[d + 1] if d + 1 < DEVS else zero)

    plain = [[it_ref[n, :, e * LANES : (e + 1) * LANES] for e in range(DEVS)] for n in range(LOCAL)]
    plain.append([coef[:, e * LANES : (e + 1) * LANES] for e in range(DEVS)])
    turned = [[flip(tile) for tile in tiles] for tiles in plain]
    turned[LOCAL] = [sign * tile for tile in turned[LOCAL]]
    for d in range(DEVS):
        tiles = turned if d % 2 else plain
        for n in range(LOCAL):
            send_ref[d, n * ROWS : (n + 1) * ROWS, :] = tiles[n][d]
        tail = [sides(tiles[n], d) for n in range(LOCAL)]
        tail.append(pltpu.roll(tiles[LOCAL][d], (ROWS - 2 * share) % ROWS, 0)[:2])
        tail.append(sides(tiles[LOCAL], d))
        send_ref[d, LOCAL * ROWS :, :] = jnp.concatenate(tail + [zero[:1]], 0)


def pieces(value):
    first = value.astype(BF16)
    rest = value - first.astype(F32)
    second = rest.astype(BF16)
    return first, second, (rest - second.astype(F32)).astype(BF16)


def stacked(table):
    one, two, three = [np.asarray(part) for part in pieces(table)]
    return np.concatenate([one, two, one, two, one, three], 1)


def mul(matrix, value):
    one, two, three = pieces(value)
    parts_of = jnp.concatenate([one, one, two, two, three, one], 0)
    return jnp.dot(matrix, parts_of, preferred_element_type=F32)


def row(refs, j):
    return refs[j // ROWS].at[j % ROWS]


def build(ref, x_ref, wt_ref, coef_ref, main_ref=None):
    def tiles(main, turned):
        lane = lane_ids(main.shape[0])
        return jnp.where(lane >= LANES - 8, turned, main), jnp.where(lane < 8, turned, main)

    def steps(offset, stride):
        starts = [half * 8 * BLOCK + n * stride + offset for n in range(LOCAL) for half in range(2)]
        return jnp.concatenate([ref[pl.ds(start, 8, stride=BLOCK), :] for start in starts], 0)

    for d in range(DEVS):
        base, share = d * BLOCK + (ROWS + 1) * LOCAL, 2 * (d // 4)
        coef_ref[d % 4, share : share + 2, :LANES] = ref[base : base + 2, :]
    rims = jnp.concatenate([steps(ROWS * LOCAL, 1), ref[pl.ds((ROWS + 1) * LOCAL + 2, 4, stride=BLOCK), :]], 0)
    for r in range(ROWS):
        main = steps(r, ROWS)
        if main_ref is not None:
            main_ref[r] = main
        turned = pltpu.roll(rims, (2 * LANES - 16 * r - 8) % LANES, 1)
        x_ref[r, DEVS:, :LANES], x_ref[r, DEVS:, LANES:] = tiles(main, turned[:STEPS])
        for a in range(4):
            one = slice(r, r + 1)
            coef_ref[a, one, :LANES], coef_ref[a, one, LANES:] = tiles(coef_ref[a, one, :LANES], turned[STEPS + a : STEPS + a + 1])
        x_ref[r, :1, :] = coef_ref[0, r : r + 1, :]
        x_ref[r, 1:DEVS, :] = x_ref[r, STEPS : STEPS + DEVS - 1, :]
    dif, cx, cy = coef_ref[1], coef_ref[2], coef_ref[3]
    west = dif + jnp.maximum(cx, 0.0)
    east = dif + jnp.maximum(-cx, 0.0)
    north = dif + jnp.maximum(cy, 0.0)
    south = dif + jnp.maximum(-cy, 0.0)
    for a, value in enumerate((west, east, north, south, west + east + north + south)):
        wt_ref[a] = value


def diagonal(shift_ref, wt_ref, a_ref, alt_ref, b_ref, r):
    centre = wt_ref[4, r : r + 1, :]
    for g in range(HALF // 8):
        part = slice(8 * g, 8 * g + 8)
        rep = lambda c: jnp.concatenate([shift_ref[part, c * LANES : (c + 1) * LANES]] * 2, 1)
        s_im = rep(1)
        d_re = rep(0) + centre
        norm = 1.0 / (d_re * d_re + s_im * s_im)
        a_ref[r, part, :] = d_re * norm
        b_ref[r, part, :] = s_im * norm
        if g == 0:
            d_im = rep(2) + centre
            alt_ref[r] = d_im * (1.0 / (d_im * d_im + s_im * s_im))


def near(wts, here, above, below):
    summed = wts[0] * pltpu.roll(here, 1, 1) + wts[1] * pltpu.roll(here, LANES - 1, 1)
    return summed + wts[2] * above + wts[3] * below


class Grid:
    def __init__(self, x, wt, a, alt, b):
        self.x, self.wt, self.a, self.alt, self.b = x, wt, a, alt, b

    def weights(self, j, cols):
        ref, r = self.wt[j // ROWS], j % ROWS
        return [ref[a, r : r + 1, cols] for a in range(5)]

    def divide(self, j, g, cols, q_re, q_im):
        part = slice(8 * g, 8 * g + 8)
        a_re, b = row(self.a, j)[part, cols], row(self.b, j)[part, cols]
        a_im = row(self.alt, j)[:, cols] if g == 0 else a_re
        return q_re * a_re + q_im * b, q_im * a_im - q_re * b

    def first(self, fwd_ref, j, dst):
        rs = []
        for cols in TILES:
            wts = self.weights(j, cols)
            here, above, below = [row(self.x, i)[DEVS:, cols] for i in (j, j - 1, j + 1)]
            rs.append(row(self.x, j)[:STEPS, cols] - here + near(wts, here, above, below) - wts[4] * here)
        hat = mul(fwd_ref[...], jnp.concatenate(rs, 1))
        for g in range(HALF // 8):
            p_re, p_im = parts(g)
            for cols in TILES:
                dst[p_re, cols], dst[p_im, cols] = self.divide(j, g, cols, hat[p_re, cols], hat[p_im, cols])

    def sweep(self, j, level, m, cols):
        values = {}
        wts = self.weights(j, cols)
        here, above, below = level(m - 1, j), level(m - 1, j - 1), level(m - 1, j + 1)
        base = level(1, j)
        for g in range(HALF // 8):
            sums = [near(wts, here[p, cols], above[p, cols], below[p, cols]) for p in parts(g)]
            for p, value in zip(parts(g), self.divide(j, g, cols, *sums)):
                values[p.start] = base[p, cols] + value
        return values

    def store(self, j, level, m, cols):
        dst = level(m, j)
        for start, value in self.sweep(j, level, m, cols).items():
            dst[start : start + 8, cols] = value


def parts(g):
    return slice(8 * g, 8 * g + 8), slice(HALF + 8 * g, HALF + 8 * g + 8)


def early(m, j):
    return (m - 2) * 4 + j - 8 - m if m in (2, 3) and 8 + m <= j < 16 - m else None


def own_kernel(
    fwd_ref, shift_ref, own_ref, main_ref, x_ref, wt_ref, a_ref, alt_ref, b_ref, f_ref, early_ref, coef_ref
):
    build(own_ref, x_ref, wt_ref, coef_ref, main_ref)
    grid = Grid(*[(None, ref, None) for ref in (x_ref, wt_ref, a_ref, alt_ref, b_ref)])
    for r in range(ROWS):
        diagonal(shift_ref, wt_ref, a_ref, alt_ref, b_ref, r)
    for r in range(1, ROWS - 1):
        grid.first(fwd_ref, ROWS + r, f_ref.at[r])

    def level(m, j):
        return f_ref.at[j - 8] if m == 1 else early_ref.at[early(m, j)]

    for m in (2, 3):
        for j in range(8 + m, 16 - m):
            for cols in TILES:
                grid.store(j, level, m, cols)


def below_kernel(
    fwd_ref, shift_ref, dn_ref, x1, wt1, a1, alt1, b1, f1, early_ref,
    f15_ref, edge_ref, x_ref, wt_ref, a_ref, alt_ref, b_ref, f_ref, w_ref, coef_ref,
):
    build(dn_ref, x_ref, wt_ref, coef_ref)
    grid = Grid((None, x1, x_ref), (None, wt1, wt_ref), (None, a1, a_ref), (None, alt1, alt_ref), (None, b1, b_ref))
    for r in range(ROWS - 1):
        diagonal(shift_ref, wt_ref, a_ref, alt_ref, b_ref, r)

    def level(m, j):
        if m == 1:
            return f1.at[j - 8] if j < 15 else f15_ref if j == 15 else f_ref.at[j - 16]
        if early(m, j) is not None:
            return early_ref.at[early(m, j)]
        return edge_ref.at[m - 4, j - 8 - m] if j <= 9 + m else w_ref.at[m % 2, j - 8]

    for j in range(15, SPAN - 1):
        grid.first(fwd_ref, j, level(1, j))
    for m in range(2, SWEEPS):
        for j in range(8 + m, SPAN - m):
            if early(m, j) is None:
                for cols in TILES:
                    grid.store(j, level, m, cols)


def last_kernel(
    t_ref, fwd_ref, inv_ref, shift_ref, up_ref, main_ref, x1, wt1, a1, alt1, b1, f1, early_ref, f15_ref, edge_ref,
    out_ref, x_ref, wt_ref, a_ref, alt_ref, b_ref, f_ref, w_ref, coef_ref,
):
    build(up_ref, x_ref, wt_ref, coef_ref)
    grid = Grid((x_ref, x1), (wt_ref, wt1), (a_ref, a1), (alt_ref, alt1), (b_ref, b1))
    for r in range(1, ROWS):
        diagonal(shift_ref, wt_ref, a_ref, alt_ref, b_ref, r)

    def level(m, j):
        if m == 1:
            return f_ref.at[j] if j <= 8 else f1.at[j - 8] if j < 15 else f15_ref
        if early(m, j) is not None:
            return early_ref.at[early(m, j)]
        return w_ref.at[m % 2, j] if j <= 7 + m else edge_ref.at[m - 4, j - 8 - m]

    for j in range(1, ROWS + 1):
        grid.first(fwd_ref, j, level(1, j))
    for m in range(2, SWEEPS):
        for j in range(m, 8 + m):
            for cols in TILES:
                grid.store(j, level, m, cols)
    lane, picked = lane_ids(8), {}
    left = lane < LANES // 2

    def pick(ref, mask=left):
        return jnp.where(mask, ref[:, TILES[0]], ref[:, TILES[1]])

    def old(j, p):
        if (j, p.start) not in picked:
            picked[j, p.start] = pick(level(SWEEPS - 1, j).at[p])
        return picked[j, p.start]

    def final(j):
        values = {}
        wts = [jnp.where(left[:1], *pair) for pair in zip(*[grid.weights(j, cols) for cols in TILES])]
        for g in range(HALF // 8):
            sums = []
            for p in parts(g):
                here = level(SWEEPS - 1, j).at[p]
                west = pltpu.roll(pick(here, left | (lane == LANES - 1)), 1, 1)
                east = pltpu.roll(pick(here, left & (lane > 0)), LANES - 1, 1)
                sums.append(wts[0] * west + wts[1] * east + wts[2] * old(j - 1, p) + wts[3] * old(j + 1, p))
            p_re, p_im = parts(g)
            a_re, b = pick(row(grid.a, j).at[p_re]), pick(row(grid.b, j).at[p_re])
            a_im = pick(row(grid.alt, j)) if g == 0 else a_re
            base = level(1, j)
            values[p_re.start] = pick(base.at[p_re]) + (sums[0] * a_re + sums[1] * b)
            values[p_im.start] = pick(base.at[p_im]) + (sums[1] * a_im - sums[0] * b)
        return jnp.concatenate([values[p] for p in range(0, STEPS, 8)], 0)

    for r in range(0, ROWS, 2):
        corr = mul(inv_ref[...], jnp.concatenate([final(ROWS + r), final(ROWS + r + 1)], 1))
        for i in range(2):
            new = main_ref[r + i] + corr[:, i * LANES : (i + 1) * LANES]
            place = jnp.where(t_ref[0] % 2 == 0, r + i, ROWS - 1 - r - i)
            for n in range(LOCAL):
                out_ref[pl.ds(n * ROWS + place, DEVS, stride=ROWS * LOCAL), :] = new[n * DEVS : (n + 1) * DEVS]


def vmem(count):
    return [pl.BlockSpec(memory_space=pltpu.VMEM)] * count


def pack(t, iterate, initial, diffusion, courant_x, courant_y):
    return pl.pallas_call(
        pack_kernel,
        name="pack",
        out_shape=pltpu.VMEM((DEVS, BLOCK, LANES), F32),
        in_specs=[pl.BlockSpec(memory_space=pltpu.SMEM)] + vmem(5),
        out_specs=vmem(1)[0],
    )(t, iterate, initial, diffusion, courant_x, courant_y)


BLOCKS = {
    "x": (ROWS, STEPS + DEVS, WIDE),
    "wt": (5, ROWS, WIDE),
    "a": (ROWS, HALF, WIDE),
    "alt": (ROWS, 8, WIDE),
    "b": (ROWS, HALF, WIDE),
}
FIELDS = (ROWS, STEPS, WIDE)
PAIRS = (SWEEPS - 4, 2, STEPS, WIDE)
EXTRA = [pltpu.VMEM((4, ROWS, WIDE), F32)]


def call(kernel, name, flops, operands, shapes, scratch, scalars=0):
    return pl.pallas_call(
        kernel,
        name=name,
        out_shape=tuple(jax.ShapeDtypeStruct(shape, F32) for shape in shapes),
        in_specs=[pl.BlockSpec(memory_space=pltpu.SMEM)] * scalars + vmem(len(operands) - scalars),
        out_specs=tuple(vmem(len(shapes))),
        scratch_shapes=[pltpu.VMEM(shape, F32) for shape in scratch] + EXTRA,
        compiler_params=pltpu.CompilerParams(vmem_limit_bytes=24 * 1024 * 1024),
        cost_estimate=pl.CostEstimate(flops=flops, bytes_accessed=2**20, transcendentals=0),
    )(*operands)


def solve(t, above, own, below):
    fwd, inv, shifts = tables()
    fwd, inv, shifts = jnp.asarray(stacked(fwd)), jnp.asarray(stacked(inv)), jnp.asarray(shifts)
    block = list(BLOCKS.values())
    main, *mine = call(own_kernel, "own", 10**7, (fwd, shifts, own), [(ROWS, STEPS, LANES)] + block + [FIELDS, (6, STEPS, WIDE)], [])
    low = call(below_kernel, "below", 2 * 10**7, (fwd, shifts, below) + tuple(mine), [(STEPS, WIDE), PAIRS], block + [FIELDS, (2, 2 * ROWS, STEPS, WIDE)])
    args = (t, fwd, inv, shifts, above, main) + tuple(mine) + tuple(low)
    return call(last_kernel, "last", 3 * 10**7, args, [(STEPS * ROWS, LANES)], block + [(ROWS + 1, STEPS, WIDE), (2, 2 * ROWS, STEPS, WIDE)], 1)[0]


def place(received):
    return received.reshape(DEVS, LOCAL, ROWS, LANES).transpose(1, 2, 0, 3).reshape(LOCAL, ROWS, DEVS * LANES)


def local(iterate, initial, diffusion, courant_x, courant_y):
    t = lax.axis_index("tm").astype(jnp.int32).reshape(1)
    send = pack(t, iterate, initial, diffusion, courant_x, courant_y)
    own = lax.all_to_all(send, "tm", split_axis=0, concat_axis=0, tiled=True)
    own = own.reshape(DEVS * BLOCK, LANES)
    count, halo = lax.axis_size("space"), []
    for way in (1, 0):
        pairs = []
        for d in range(DEVS):
            for i in range(count - 1):
                lower, upper = d * count + i + 1, d * count + i
                pairs.append((upper, lower) if d % 2 == way else (lower, upper))
        halo.append(lax.ppermute(own, ("tm", "space"), pairs))
    below, above = halo
    new = solve(t, above, own, below)
    back = lax.all_to_all(new.reshape(DEVS, LOCAL * ROWS, LANES), "tm", split_axis=0, concat_axis=0, tiled=True)
    return place(back)


def solution(mesh):
    return jax.shard_map(
        local,
        mesh=mesh,
        in_specs=(
            P("tm", "space", None),
            P("space", None),
            P("space", None),
            P("space", None),
            P("space", None),
        ),
        out_specs=P("tm", "space", None),
        check_vma=False,
    )
```

```python
import math

import jax
import jax.numpy as jnp
import numpy as np
from jax import lax
from jax.experimental import pallas as pl
from jax.experimental.pallas import tpu as pltpu
from jax.sharding import PartitionSpec as P

SWEEPS = 8
ALPHA = 0.01
STEPS = 64
HALF = STEPS // 2
DEVS = 16
LOCAL = STEPS // DEVS
ROWS = 8
LANES = 128
BLOCK = ROWS * LOCAL + ROWS
SPAN = 3 * ROWS
WIDE = 2 * LANES
TILES = (slice(0, LANES), slice(LANES, WIDE))
F32 = jnp.float32
BF16 = jnp.bfloat16


def tables():
    n = np.arange(STEPS)
    g = ALPHA ** (n / STEPS)
    k = np.arange(HALF)
    ang = 2.0 * np.pi * (np.outer(k, n) % STEPS) / STEPS
    fwd = np.concatenate([np.cos(ang) * g, -np.sin(ang) * g], 0)
    fwd[HALF] = (-1.0) ** n * g
    inv = np.concatenate([2.0 * np.cos(ang), -2.0 * np.sin(ang)], 0).T
    inv[:, 0] = 1.0
    inv[:, HALF] = (-1.0) ** n
    inv = inv / (STEPS * g[:, None])
    beta = ALPHA ** (1.0 / STEPS)
    shift_re = 1.0 - beta * np.cos(2.0 * np.pi * k / STEPS)
    shift_im = beta * np.sin(2.0 * np.pi * k / STEPS)
    shift_alt = shift_re.copy()
    shift_alt[0] = 1.0 + beta
    order = n.reshape(DEVS, LOCAL).T.reshape(-1)
    fwd, inv = fwd[:, order], inv[order]
    shifts = np.zeros((HALF, 3 * LANES), np.float32)
    shifts[:, :LANES] = shift_re[:, None]
    shifts[:, LANES : 2 * LANES] = shift_im[:, None]
    shifts[:, 2 * LANES :] = shift_alt[:, None]
    return fwd.astype(np.float32), inv.astype(np.float32), shifts


def lane_ids(rows):
    return lax.broadcasted_iota(jnp.int32, (rows, LANES), 1)


def rim(left, right):
    lane = lane_ids(ROWS)
    both = jnp.where(lane < 8, right, jnp.where(lane >= LANES - 8, left, 0.0))
    moved = pltpu.roll(both, 8, 1, stride=16, stride_axis=0)
    return jnp.sum(moved, axis=0, keepdims=True)


def flip(tile):
    row = lax.broadcasted_iota(jnp.int32, (ROWS, LANES), 0)
    return jnp.take_along_axis(tile, ROWS - 1 - row, axis=0)


def pack_kernel(t_ref, it_ref, ini_ref, dif_ref, cx_ref, cy_ref, send_ref):
    t = t_ref[0]
    which, share = t % 4, t // 4
    coef = jnp.where(which < 2, jnp.where(which == 0, ini_ref[...], dif_ref[...]), jnp.where(which == 2, cx_ref[...], cy_ref[...]))
    sign = jnp.where(which == 3, -1.0, 1.0)
    zero = jnp.zeros((ROWS, LANES), F32)

    def sides(tiles, d):
        return rim(tiles[d - 1] if d else zero, tiles[d + 1] if d + 1 < DEVS else zero)

    plain = [[it_ref[n, :, e * LANES : (e + 1) * LANES] for e in range(DEVS)] for n in range(LOCAL)]
    plain.append([coef[:, e * LANES : (e + 1) * LANES] for e in range(DEVS)])
    turned = [[flip(tile) for tile in tiles] for tiles in plain]
    turned[LOCAL] = [sign * tile for tile in turned[LOCAL]]
    odd = t_ref[1] % 2 == 1
    pick = lambda one, two: [[jnp.where(odd, b, a) for a, b in zip(*rows)] for rows in zip(one, two)]
    sets = pick(plain, turned), pick(turned, plain)
    for d in range(DEVS):
        tiles = sets[d % 2]
        for n in range(LOCAL):
            send_ref[d, n * ROWS : (n + 1) * ROWS, :] = tiles[n][d]
        tail = [sides(tiles[n], d) for n in range(LOCAL)]
        tail.append(pltpu.roll(tiles[LOCAL][d], (ROWS - 2 * share) % ROWS, 0)[:2])
        tail.append(sides(tiles[LOCAL], d))
        send_ref[d, LOCAL * ROWS :, :] = jnp.concatenate(tail + [zero[:1]], 0)


def pieces(value):
    first = value.astype(BF16)
    rest = value - first.astype(F32)
    second = rest.astype(BF16)
    return first, second, (rest - second.astype(F32)).astype(BF16)


def stacked(table):
    one, two, three = [np.asarray(part) for part in pieces(table)]
    return np.concatenate([one, two, one, two, one, three], 1)


def mul(matrix, value):
    one, two, three = pieces(value)
    parts_of = jnp.concatenate([one, one, two, two, three, one], 0)
    return jnp.dot(matrix, parts_of, preferred_element_type=F32)


def row(refs, j):
    return refs[j // ROWS].at[j % ROWS]


def build(ref, x_ref, wt_ref, coef_ref, main_ref=None, mirrored=False):
    def tiles(main, turned):
        lane = lane_ids(main.shape[0])
        return jnp.where(lane >= LANES - 8, turned, main), jnp.where(lane < 8, turned, main)

    def steps(offset, stride):
        starts = [half * 8 * BLOCK + n * stride + offset for n in range(LOCAL) for half in range(2)]
        return jnp.concatenate([ref[pl.ds(start, 8, stride=BLOCK), :] for start in starts], 0)

    for d in range(DEVS):
        base, share = d * BLOCK + (ROWS + 1) * LOCAL, 2 * (d // 4)
        coef_ref[d % 4, share : share + 2, :LANES] = ref[base : base + 2, :]
    rims = jnp.concatenate([steps(ROWS * LOCAL, 1), ref[pl.ds((ROWS + 1) * LOCAL + 2, 4, stride=BLOCK), :]], 0)
    if mirrored:
        for a in range(4):
            coef_ref[a, :, :LANES] = flip(coef_ref[a, :, :LANES])
    for r in range(ROWS):
        source = ROWS - 1 - r if mirrored else r
        main = steps(source, ROWS)
        if main_ref is not None:
            main_ref[r] = main
        turned = pltpu.roll(rims, (2 * LANES - 16 * source - 8) % LANES, 1)
        x_ref[r, DEVS:, :LANES], x_ref[r, DEVS:, LANES:] = tiles(main, turned[:STEPS])
        for a in range(4):
            one = slice(r, r + 1)
            coef_ref[a, one, :LANES], coef_ref[a, one, LANES:] = tiles(coef_ref[a, one, :LANES], turned[STEPS + a : STEPS + a + 1])
        x_ref[r, :1, :] = coef_ref[0, r : r + 1, :]
        x_ref[r, 1:DEVS, :] = x_ref[r, STEPS : STEPS + DEVS - 1, :]
    dif, cx, cy = coef_ref[1], coef_ref[2], coef_ref[3]
    cy = -cy if mirrored else cy
    west = dif + jnp.maximum(cx, 0.0)
    east = dif + jnp.maximum(-cx, 0.0)
    north = dif + jnp.maximum(cy, 0.0)
    south = dif + jnp.maximum(-cy, 0.0)
    for a, value in enumerate((west, east, north, south, west + east + north + south)):
        wt_ref[a] = value


def diagonal(shift_ref, wt_ref, a_ref, alt_ref, b_ref, r):
    centre = wt_ref[4, r : r + 1, :]
    for g in range(HALF // 8):
        part = slice(8 * g, 8 * g + 8)
        rep = lambda c: jnp.concatenate([shift_ref[part, c * LANES : (c + 1) * LANES]] * 2, 1)
        s_im = rep(1)
        d_re = rep(0) + centre
        norm = 1.0 / (d_re * d_re + s_im * s_im)
        a_ref[r, part, :] = d_re * norm
        b_ref[r, part, :] = s_im * norm
        if g == 0:
            d_im = rep(2) + centre
            alt_ref[r] = d_im * (1.0 / (d_im * d_im + s_im * s_im))


def near(wts, here, above, below):
    summed = wts[0] * pltpu.roll(here, 1, 1) + wts[1] * pltpu.roll(here, LANES - 1, 1)
    return summed + wts[2] * above + wts[3] * below


class Grid:
    def __init__(self, x, wt, a, alt, b):
        self.x, self.wt, self.a, self.alt, self.b = x, wt, a, alt, b

    def weights(self, j, cols):
        ref, r = self.wt[j // ROWS], j % ROWS
        return [ref[a, r : r + 1, cols] for a in range(5)]

    def divide(self, j, g, cols, q_re, q_im):
        part = slice(8 * g, 8 * g + 8)
        a_re, b = row(self.a, j)[part, cols], row(self.b, j)[part, cols]
        a_im = row(self.alt, j)[:, cols] if g == 0 else a_re
        return q_re * a_re + q_im * b, q_im * a_im - q_re * b

    def first(self, fwd_ref, j, dst):
        rs = []
        for cols in TILES:
            wts = self.weights(j, cols)
            here, above, below = [row(self.x, i)[DEVS:, cols] for i in (j, j - 1, j + 1)]
            rs.append(row(self.x, j)[:STEPS, cols] - here + near(wts, here, above, below) - wts[4] * here)
        hat = mul(fwd_ref[...], jnp.concatenate(rs, 1))
        for g in range(HALF // 8):
            p_re, p_im = parts(g)
            for cols in TILES:
                dst[p_re, cols], dst[p_im, cols] = self.divide(j, g, cols, hat[p_re, cols], hat[p_im, cols])

    def sweep(self, j, level, m, cols):
        values = {}
        wts = self.weights(j, cols)
        here, above, below = level(m - 1, j), level(m - 1, j - 1), level(m - 1, j + 1)
        base = level(1, j)
        for g in range(HALF // 8):
            sums = [near(wts, here[p, cols], above[p, cols], below[p, cols]) for p in parts(g)]
            for p, value in zip(parts(g), self.divide(j, g, cols, *sums)):
                values[p.start] = base[p, cols] + value
        return values

    def store(self, j, level, m, cols):
        dst = level(m, j)
        for start, value in self.sweep(j, level, m, cols).items():
            dst[start : start + 8, cols] = value


def parts(g):
    return slice(8 * g, 8 * g + 8), slice(HALF + 8 * g, HALF + 8 * g + 8)


def early(m, j):
    return (m - 2) * 4 + j - 8 - m if m in (2, 3) and 8 + m <= j < 16 - m else None


def own_kernel(
    fwd_ref, shift_ref, own_ref, main_ref, x_ref, wt_ref, a_ref, alt_ref, b_ref, f_ref, early_ref, coef_ref
):
    build(own_ref, x_ref, wt_ref, coef_ref, main_ref)
    grid = Grid(*[(None, ref, None) for ref in (x_ref, wt_ref, a_ref, alt_ref, b_ref)])
    for r in range(ROWS):
        diagonal(shift_ref, wt_ref, a_ref, alt_ref, b_ref, r)
    for r in range(1, ROWS - 1):
        grid.first(fwd_ref, ROWS + r, f_ref.at[r])

    def level(m, j):
        return f_ref.at[j - 8] if m == 1 else early_ref.at[early(m, j)]

    for m in (2, 3):
        for j in range(8 + m, 16 - m):
            for cols in TILES:
                grid.store(j, level, m, cols)


def below_kernel(
    fwd_ref, shift_ref, dn_ref, x1, wt1, a1, alt1, b1, f1, early_ref,
    f15_ref, edge_ref, x_ref, wt_ref, a_ref, alt_ref, b_ref, f_ref, w_ref, coef_ref,
):
    build(dn_ref, x_ref, wt_ref, coef_ref, mirrored=True)
    grid = Grid((None, x1, x_ref), (None, wt1, wt_ref), (None, a1, a_ref), (None, alt1, alt_ref), (None, b1, b_ref))
    for r in range(ROWS - 1):
        diagonal(shift_ref, wt_ref, a_ref, alt_ref, b_ref, r)

    def level(m, j):
        if m == 1:
            return f1.at[j - 8] if j < 15 else f15_ref if j == 15 else f_ref.at[j - 16]
        if early(m, j) is not None:
            return early_ref.at[early(m, j)]
        return edge_ref.at[m - 4, j - 8 - m] if j <= 9 + m else w_ref.at[m % 2, j - 8]

    for j in range(15, SPAN - 1):
        grid.first(fwd_ref, j, level(1, j))
    for m in range(2, SWEEPS):
        for j in range(8 + m, SPAN - m):
            if early(m, j) is None:
                for cols in TILES:
                    grid.store(j, level, m, cols)


def last_kernel(
    t_ref, fwd_ref, inv_ref, shift_ref, up_ref, main_ref, x1, wt1, a1, alt1, b1, f1, early_ref, f15_ref, edge_ref,
    out_ref, x_ref, wt_ref, a_ref, alt_ref, b_ref, f_ref, w_ref, coef_ref,
):
    build(up_ref, x_ref, wt_ref, coef_ref, mirrored=True)
    grid = Grid((x_ref, x1), (wt_ref, wt1), (a_ref, a1), (alt_ref, alt1), (b_ref, b1))
    for r in range(1, ROWS):
        diagonal(shift_ref, wt_ref, a_ref, alt_ref, b_ref, r)

    def level(m, j):
        if m == 1:
            return f_ref.at[j] if j <= 8 else f1.at[j - 8] if j < 15 else f15_ref
        if early(m, j) is not None:
            return early_ref.at[early(m, j)]
        return w_ref.at[m % 2, j] if j <= 7 + m else edge_ref.at[m - 4, j - 8 - m]

    for j in range(1, ROWS + 1):
        grid.first(fwd_ref, j, level(1, j))
    for m in range(2, SWEEPS):
        for j in range(m, 8 + m):
            for cols in TILES:
                grid.store(j, level, m, cols)
    lane, picked = lane_ids(8), {}
    left = lane < LANES // 2
    odd = t_ref[2]

    def pick(ref, mask=left):
        return jnp.where(mask, ref[:, TILES[0]], ref[:, TILES[1]])

    def old(j, p):
        if (j, p.start) not in picked:
            picked[j, p.start] = pick(level(SWEEPS - 1, j).at[p])
        return picked[j, p.start]

    def final(j):
        values = {}
        wts = [jnp.where(left[:1], *pair) for pair in zip(*[grid.weights(j, cols) for cols in TILES])]
        for g in range(HALF // 8):
            sums = []
            for p in parts(g):
                here = level(SWEEPS - 1, j).at[p]
                west = pltpu.roll(pick(here, left | (lane == LANES - 1)), 1, 1)
                east = pltpu.roll(pick(here, left & (lane > 0)), LANES - 1, 1)
                sums.append(wts[0] * west + wts[1] * east + wts[2] * old(j - 1, p) + wts[3] * old(j + 1, p))
            p_re, p_im = parts(g)
            a_re, b = pick(row(grid.a, j).at[p_re]), pick(row(grid.b, j).at[p_re])
            a_im = pick(row(grid.alt, j)) if g == 0 else a_re
            base = level(1, j)
            values[p_re.start] = pick(base.at[p_re]) + (sums[0] * a_re + sums[1] * b)
            values[p_im.start] = pick(base.at[p_im]) + (sums[1] * a_im - sums[0] * b)
        return jnp.concatenate([values[p] for p in range(0, STEPS, 8)], 0)

    for r in range(0, ROWS, 2):
        corr = mul(inv_ref[...], jnp.concatenate([final(ROWS + r), final(ROWS + r + 1)], 1))
        for i in range(2):
            new = main_ref[r + i] + corr[:, i * LANES : (i + 1) * LANES]
            place = r + i + odd * (ROWS - 1 - 2 * (r + i))
            for n in range(LOCAL):
                out_ref[pl.ds(n * ROWS + place, DEVS, stride=ROWS * LOCAL), :] = new[n * DEVS : (n + 1) * DEVS]


def vmem(count):
    return [pl.BlockSpec(memory_space=pltpu.VMEM)] * count


def pack(t, iterate, initial, diffusion, courant_x, courant_y):
    return pl.pallas_call(
        pack_kernel,
        name="pack",
        out_shape=pltpu.VMEM((DEVS, BLOCK, LANES), F32),
        in_specs=[pl.BlockSpec(memory_space=pltpu.SMEM)] + vmem(5),
        out_specs=vmem(1)[0],
    )(t, iterate, initial, diffusion, courant_x, courant_y)


BLOCKS = {
    "x": (ROWS, STEPS + DEVS, WIDE),
    "wt": (5, ROWS, WIDE),
    "a": (ROWS, HALF, WIDE),
    "alt": (ROWS, 8, WIDE),
    "b": (ROWS, HALF, WIDE),
}
FIELDS = (ROWS, STEPS, WIDE)
PAIRS = (SWEEPS - 4, 2, STEPS, WIDE)
EXTRA = [pltpu.VMEM((4, ROWS, WIDE), F32)]


def call(kernel, name, flops, operands, shapes, scratch, scalars=0):
    return pl.pallas_call(
        kernel,
        name=name,
        out_shape=tuple(jax.ShapeDtypeStruct(shape, F32) for shape in shapes),
        in_specs=[pl.BlockSpec(memory_space=pltpu.SMEM)] * scalars + vmem(len(operands) - scalars),
        out_specs=tuple(vmem(len(shapes))),
        scratch_shapes=[pltpu.VMEM(shape, F32) for shape in scratch] + EXTRA,
        compiler_params=pltpu.CompilerParams(vmem_limit_bytes=24 * 1024 * 1024),
        cost_estimate=pl.CostEstimate(flops=flops, bytes_accessed=2**20, transcendentals=0),
    )(*operands)


def solve(t, above, own, below):
    fwd, inv, shifts = tables()
    fwd, inv, shifts = jnp.asarray(stacked(fwd)), jnp.asarray(stacked(inv)), jnp.asarray(shifts)
    block = list(BLOCKS.values())
    main, *mine = call(own_kernel, "own", 10**7, (fwd, shifts, own), [(ROWS, STEPS, LANES)] + block + [FIELDS, (6, STEPS, WIDE)], [])
    low = call(below_kernel, "below", 2 * 10**7, (fwd, shifts, below) + tuple(mine), [(STEPS, WIDE), PAIRS], block + [FIELDS, (2, 2 * ROWS, STEPS, WIDE)])
    args = (t, fwd, inv, shifts, above, main) + tuple(mine) + tuple(low)
    return call(last_kernel, "last", 3 * 10**7, args, [(STEPS * ROWS, LANES)], block + [(ROWS + 1, STEPS, WIDE), (2, 2 * ROWS, STEPS, WIDE)], 1)[0]


def place(received):
    return received.reshape(DEVS, LOCAL, ROWS, LANES).transpose(1, 2, 0, 3).reshape(LOCAL, ROWS, DEVS * LANES)


def local(iterate, initial, diffusion, courant_x, courant_y):
    t, s = lax.axis_index("tm"), lax.axis_index("space")
    t = jnp.stack([t, s, (t + s) % 2]).astype(jnp.int32)
    send = pack(t, iterate, initial, diffusion, courant_x, courant_y)
    own = lax.all_to_all(send, "tm", split_axis=0, concat_axis=0, tiled=True)
    own = own.reshape(DEVS * BLOCK, LANES)
    count, halo = lax.axis_size("space"), []
    for way in (0, 1):
        pairs = []
        for d in range(DEVS):
            for i in range(count - 1):
                if (i + d) % 2 == way:
                    one, two = d * count + i, d * count + i + 1
                    pairs += [(one, two), (two, one)]
        halo.append(lax.ppermute(own, ("tm", "space"), pairs))
    below, above = halo
    new = solve(t, above, own, below)
    back = lax.all_to_all(new.reshape(DEVS, LOCAL * ROWS, LANES), "tm", split_axis=0, concat_axis=0, tiled=True)
    return place(back)


def solution(mesh):
    return jax.shard_map(
        local,
        mesh=mesh,
        in_specs=(
            P("tm", "space", None),
            P("space", None),
            P("space", None),
            P("space", None),
            P("space", None),
        ),
        out_specs=P("tm", "space", None),
        check_vma=False,
    )
```
